256 devices in a mesh: dp: 32 (over y_lo, z, core), tensor: 8 (over y_hi, x).
Axes of the slice: x: 4, y: 4 (y_hi: 2, y_lo: 2; y = y_hi * 2 + y_lo), z: 8, core: 2. Of those that a mesh axis runs over, the one named last changes fastest.
Arguments:
- context: bfloat16 [49152, 5120], P(('dp', 'tensor')), may hold values from -6 to 6
- residual: bfloat16 [49152, 10240], P(('dp', 'tensor')), may hold values from -128 to 128
- out_weight: bfloat16 [5120, 10240], P('dp', 'tensor'), may hold values from -0.078125 to 0.078125
- norm_gain: float32 [10240], P('tensor'), may hold values from 0.5 to 1.5
- norm_bias: float32 [10240], P('tensor'), may hold values from -3 to 3
- head_weight: bfloat16 [10240, 128], P('tensor'), may hold values from -0.207524471 to 0.207524471
- targets: int32 [49152], P(('dp', 'tensor')), may hold values from 0 to 127
- packing: int32 [2, 49152], P(None, ('dp', 'tensor')), may hold values from -1 to 95, as said below
- lengths: int32 [1024], P(('dp', 'tensor')), may hold values from 0 to 192, as said below
Outputs:
- residue_scores: float32 [49152], P(('dp', 'tensor'))
- packed_scores: float32 [24576], P(('dp', 'tensor'))
- protein_scores: float32 [1024], P(('dp', 'tensor'))
The draws below stay inside these ranges and needn't reach their ends.
Inputs may be any that keep to these rules, and one draw needn't show every extreme that they name: Row r of owner block d = r // 192 (blocks in mesh order, dp slowest) is live where packing[0, r] >= 0, and then goes to data group packing[0, r] in lane d % 8 at packed row packing[1, r]; dead rows hold -1 in both. Live rows of a block come first, their count is 0 to 192 with both ends reached. Every packed row of every group and lane receives exactly one live row. From one owner block to one group at most 6 rows, reached in every draw. The 4 lengths of a block sum to the block's count of live rows; a length may be 0.
All inputs are finite; a program needn't handle non-finite values.
Results may differ from the reference program's by a relative error of at most 0.0003.
Values may be sent and summed in bfloat16 or wider, within the bound.
A program may use at most 128 MiB of HBM per device.

```python
import jax
import jax.numpy as jnp
from jax import lax

D = 10240
VOCAB = 128
GROUP_DEV = 96
PROT_DEV = 4
CTX = 5120
OWN_DEV = 192
OWN_ALL = 49152
GROUP_ALL = 24576
PROT_ALL = 1024
N_DP = 32
N_TENSOR = 8
DEVICES = 256


def head_matrix(key):
    values = jax.random.normal(jax.random.fold_in(key, 11), (D, VOCAB), jnp.float32)
    return jnp.clip(values, -6.0, 6.0) * (3.5 / D ** 0.5)


def owner_plan(key):
    base_key = jax.random.fold_in(key, 7)
    order_key, shift_key, cut_key = jax.random.split(base_key, 3)
    orders = jax.vmap(lambda single: jax.random.permutation(single, N_DP))(jax.random.split(order_key, N_TENSOR))
    half_count = N_DP // 2
    shifts = jax.random.randint(shift_key, (N_TENSOR, half_count), 0, GROUP_DEV + 1)
    shifts = shifts.at[:, 0].set(GROUP_DEV)
    lane_rows = jnp.arange(N_TENSOR)[:, None]
    counts = jnp.zeros((N_TENSOR, N_DP), jnp.int32)
    counts = counts.at[lane_rows, orders[:, :half_count]].set(GROUP_DEV + shifts)
    counts = counts.at[lane_rows, orders[:, half_count:]].set(GROUP_DEV - shifts)
    before = jnp.cumsum(counts, axis=1) - counts
    positions = jnp.arange(OWN_DEV, dtype=jnp.int32)
    global_rank = before.T[:, :, None] + positions[None, None, :]
    live_mask = positions[None, None, :] < counts.T[:, :, None]
    groups = jnp.where(live_mask, global_rank % N_DP, -1)
    offsets = jnp.where(live_mask, global_rank // N_DP, -1)
    packing = jnp.stack([groups.reshape(-1), offsets.reshape(-1)]).astype(jnp.int32)
    limits = counts.T[:, :, None]
    cut_points = jnp.sort(jax.random.randint(cut_key, (N_DP, N_TENSOR, PROT_DEV - 1), 0, limits + 1), axis=2)
    full_block = (jnp.arange(N_DP)[:, None, None] == orders[0, 0]) & (jnp.arange(N_TENSOR)[None, :, None] == 0)
    cut_points = jnp.where(full_block, limits, cut_points)
    end_points = jnp.concatenate([cut_points, limits], axis=2)
    start_points = jnp.concatenate([jnp.zeros_like(limits), cut_points], axis=2)
    lengths = (end_points - start_points).reshape(-1).astype(jnp.int32)
    return (packing, lengths)


def draw_packing(key, part):
    return owner_plan(key)[0]


def draw_lengths(key, part):
    return owner_plan(key)[1]


def draw_head_weight(key, part):
    return head_matrix(key).astype(jnp.bfloat16)


def draw_residual(key, part):
    own_key = jax.random.fold_in(key, 3)
    row_key, col_key, noise_key, shift_key = jax.random.split(own_key, 4)
    total_rows = OWN_ALL
    row_scale = jnp.exp(jax.random.uniform(row_key, (total_rows, 1)) * jnp.log(10.0)) * 0.5
    column_place = jnp.arange(D, dtype=jnp.float32)[None, :] / D
    column_scale = 3.0 ** column_place / 2.0 * jax.random.uniform(col_key, (1, D), minval=0.6, maxval=1.6)
    noise_values = jnp.clip(jax.random.normal(noise_key, (total_rows, D)), -6.0, 6.0)
    column_shift = jax.random.uniform(shift_key, (1, D), minval=-1.0, maxval=1.0)
    values = row_scale * (column_scale * noise_values + 0.5 * column_shift)
    return jnp.clip(values, -128.0, 128.0).astype(jnp.bfloat16)


def set_ends(drawn, stream_key, smallest, high):
    shape = drawn.shape
    place = [jax.random.randint(jax.random.fold_in(stream_key, axis), (), 0, shape[axis]) for axis in range(len(shape))]
    drawn = drawn.at[tuple(place)].set(smallest)
    longest = shape.index(max(shape))
    place[longest] = (place[longest] + 1) % shape[longest]
    return drawn.at[tuple(place)].set(high)


def shard_levels(stream_key, extent, cuts, least, high):
    factor_of, own = 1.0, jax.random.fold_in(stream_key, 6)
    for axis_at, parts in cuts:
        heights = jnp.exp(jax.random.uniform(jax.random.fold_in(own, axis_at), (parts,), jnp.float32, least / len(cuts), high / len(cuts)))
        factor_of = factor_of * jnp.repeat(heights, extent[axis_at] // parts).reshape([-1 if axis == axis_at else 1 for axis in range(len(extent))])
    return factor_of


def bell_draw(key, shape, width, bound, pieces=(), kind=jnp.bfloat16):
    level = shard_levels(key, shape, pieces, -0.22, 0.18) if pieces else 1.0
    array = jax.random.normal(key, shape, jnp.float32) * width * level
    return jnp.minimum(jnp.maximum(array, -bound), bound).astype(kind)


def setup_inputs(seed: int = 0) -> dict:
    key_of = jax.random.split(jax.random.key(seed), 10)
    return {
        "context": bell_draw(key_of[0], (OWN_ALL, CTX), 1.0, 6.0, ((0, 256),)),
        "residual": draw_residual(jax.random.fold_in(key_of[9], 71), 0),
        "out_weight": bell_draw(key_of[2], (CTX, D), CTX ** -0.5, 0.078125, ((0, 32), (1, 8))),
        "norm_gain": jnp.clip(1.0 + 0.1 * jax.random.normal(key_of[3], (D,), jnp.float32), 0.5, 1.5),
        "norm_bias": bell_draw(key_of[4], (D,), 0.5, 3.0, ((0, 8),), jnp.float32),
        "head_weight": draw_head_weight(jax.random.fold_in(key_of[9], 71), 0),
        "targets": set_ends(jax.random.randint(key_of[6], (OWN_ALL,), 0, VOCAB), jax.random.fold_in(key_of[6], 1), 0, VOCAB - 1).astype(jnp.int32),
        "packing": draw_packing(jax.random.fold_in(key_of[9], 71), 0),
        "lengths": draw_lengths(jax.random.fold_in(key_of[9], 71), 0),
    }


epsilon = 1e-05

def score_block(ctx_block, resid_block, target_block, out_weight, norm_gain, norm_bias, head_float):
    hidden = resid_block.astype(jnp.float32) + jnp.dot(ctx_block, out_weight, preferred_element_type=jnp.float32)
    center = lax.optimization_barrier(jnp.mean(hidden, axis=1, keepdims=True))
    spread = lax.optimization_barrier(jnp.mean((hidden - center) ** 2, axis=1, keepdims=True))
    normed = (hidden - center) * lax.rsqrt(spread + epsilon) * norm_gain.astype(jnp.float32) + norm_bias.astype(jnp.float32)
    logits = jnp.dot(normed, head_float, precision=lax.Precision.HIGHEST)
    largest = lax.optimization_barrier(jnp.max(logits, axis=1, keepdims=True))
    log_total = largest[:, 0] + jnp.log(lax.optimization_barrier(jnp.sum(jnp.exp(logits - largest), axis=1)))
    token_ids = jnp.arange(logits.shape[1], dtype=jnp.int32)
    picked = lax.optimization_barrier(jnp.sum(jnp.where(token_ids[None, :] == target_block[:, None], logits, 0.0), axis=1))
    return picked - log_total

def reference(context, residual, out_weight, norm_gain, norm_bias, head_weight, targets, packing, lengths):
    total_rows = context.shape[0]
    row_index = jnp.arange(total_rows, dtype=jnp.int32)
    lane_index = row_index // OWN_DEV % N_TENSOR
    live_rows = packing[0] >= 0
    packed_slot = jnp.where(live_rows, (packing[0] * N_TENSOR + lane_index) * GROUP_DEV + packing[1], GROUP_ALL).astype(jnp.int32)
    source_row = jnp.zeros((GROUP_ALL + 1,), jnp.int32).at[packed_slot].set(row_index)[:GROUP_ALL]
    head_float = head_weight.astype(jnp.float32)
    block_rows = GROUP_DEV * N_TENSOR
    source_blocks = source_row.reshape(GROUP_ALL // block_rows, block_rows)

    def one_block(pick_rows):
        return score_block(context[pick_rows], residual[pick_rows], targets[pick_rows], out_weight, norm_gain, norm_bias, head_float)
    packed_scores = lax.map(one_block, source_blocks).reshape(GROUP_ALL)
    safe_slot = jnp.minimum(packed_slot, GROUP_ALL - 1).astype(jnp.int32)
    residue_scores = jnp.where(live_rows, packed_scores[safe_slot], 0.0)
    per_device = residue_scores.reshape(DEVICES, OWN_DEV)
    size_table = lengths.reshape(DEVICES, PROT_DEV)
    end_rows = jnp.cumsum(size_table, axis=1)
    start_rows = end_rows - size_table
    positions = jnp.arange(OWN_DEV, dtype=jnp.int32)
    member = ((positions[None, None, :] >= start_rows[:, :, None]) & (positions[None, None, :] < end_rows[:, :, None])).astype(jnp.float32)
    protein_sums = jnp.einsum('dpr,dr->dp', member, per_device, precision=lax.Precision.HIGHEST)
    protein_scores = (protein_sums / jnp.maximum(size_table, 1).astype(jnp.float32)).reshape(PROT_ALL)
    return (residue_scores, packed_scores, protein_scores)
```

```python
import jax
import jax.numpy as jnp
from jax import lax
from jax.experimental import pallas as pl
from jax.experimental.pallas import tpu as pltpu
from jax.sharding import PartitionSpec as P

MESH = pl.DeviceIdType.MESH
F32 = jnp.float32
BF16 = jnp.bfloat16
EPS = 1e-05
NX, NZ, NDP = 4, 8, 32
ROWS, HALF = 192, 96
KB, NB, CTX, VOCAB = 160, 1280, 5120, 128
LOCAL_WIDTH = 2 * NB
WIDTH = NX * LOCAL_WIDTH
PAIR = 4 * KB


def kernel(
    ctx, res, w, head, gain, bias, info, lens,
    res_out, pk_out, pr_out,
    ctx_all, res_in, transit, w_all, hid, head_all, gain_all, bias_all,
    g_own, g_in, part, part_in, dp_send, dp_in,
    lsem, cs, cr, rs, rr, ws, wr, zs, zr, hs, hr, ns, nr, gs, gr, ps, pr, ds_, dr,
):
    dp = lax.axis_index("dp")
    tensor = lax.axis_index("tensor")
    core = lax.rem(dp, 2)
    z = lax.rem(dp // 2, NZ)
    yl = dp // (2 * NZ)
    x = lax.rem(tensor, NX)
    yh = tensor // NX
    y = yh * 2 + yl

    def x_dev(k):
        return (dp, yh * NX + lax.rem(x + k, NX))

    def y_dev(k):
        to = lax.rem(y + k, 4)
        return ((lax.rem(to, 2) * NZ + z) * 2 + core, (to // 2) * NX + x)

    def z_dev(k):
        return ((yl * NZ + lax.rem(z + k, NZ)) * 2 + core, tensor)

    sibling = (dp + 1 - 2 * core, tensor)
    left, right = lax.rem(x + 3, NX), lax.rem(x + 1, NX)

    def send(src, dst, ssem, rsem, dev):
        copy = pltpu.make_async_remote_copy(
            src_ref=src, dst_ref=dst, send_sem=ssem, recv_sem=rsem,
            device_id=dev, device_id_type=MESH,
        )
        copy.start()
        return copy

    def arrived(ref, sem):
        pltpu.make_async_copy(ref, ref, sem).wait()

    barrier = pltpu.get_barrier_semaphore()

    @pl.loop(1, NDP)
    def _(k):
        pl.semaphore_signal(barrier, inc=1, device_id=(lax.rem(dp + k, NDP), tensor), device_id_type=MESH)

    for k in (1, 2, 3):
        pl.semaphore_signal(barrier, inc=1, device_id=x_dev(k), device_id_type=MESH)
    for other in (yl, 1 - yl):
        pl.semaphore_signal(
            barrier, inc=1, device_id=((other * NZ + z) * 2 + core, (1 - yh) * NX + x), device_id_type=MESH
        )
    pl.semaphore_wait(barrier, NDP - 1 + 5)

    mine = w_all.at[yh, yl, z, core]
    w_out = [send(w, mine, ws.at[k - 1], wr.at[k - 1], y_dev(k)) for k in (1, 2, 3)]
    w_own = pltpu.make_async_copy(w, mine, lsem.at[0])
    w_own.start()

    def ctx_part(ref, part_of):
        return ref.at[pl.ds(part_of * HALF, HALF)]

    c_out = []

    def send_ctx(way, part_of):
        at = way * 2 + part_of
        c_out.append(
            send(
                ctx_part(ctx, part_of), ctx_part(ctx_all.at[x], part_of), cs.at[at], cr.at[at],
                x_dev(1 if way == 0 else 3),
            )
        )

    def columns(block, to):
        return pl.ds(pl.multiple_of((block * NX + to) * NB, NB), NB)

    opposite = lax.rem(x + 2, NX)
    r_out = []
    send_ctx(0, 0)
    send_ctx(1, 1)
    for way in (0, 1):
        for block in (0, 1):
            at = way * 2 + block
            r_out.append(
                send(
                    res.at[pl.ds(way * HALF, HALF), columns(block, opposite)], transit.at[way, block],
                    rs.at[at], rr.at[at], x_dev(1 if way == 0 else 3),
                )
            )
    send_ctx(0, 1)
    send_ctx(1, 0)
    for way in (0, 1):
        for block in (0, 1):
            at = 4 + way * 2 + block
            r_out.append(
                send(
                    res.at[:, columns(block, right if way == 0 else left)], res_in.at[x, block],
                    rs.at[at], rr.at[at], x_dev(1 if way == 0 else 3),
                )
            )
    partner = y_dev(2)
    n_out = [
        send(head, head_all.at[yh], ns.at[0], nr.at[0], partner),
        send(gain, gain_all.at[yh], ns.at[1], nr.at[1], partner),
        send(bias, bias_all.at[yh], ns.at[2], nr.at[2], partner),
    ]
    own = [
        pltpu.make_async_copy(ctx, ctx_all.at[x], lsem.at[1]),
        pltpu.make_async_copy(res.at[:, columns(0, x)], res_in.at[x, 0], lsem.at[2]),
        pltpu.make_async_copy(res.at[:, columns(1, x)], res_in.at[x, 1], lsem.at[3]),
        pltpu.make_async_copy(head, head_all.at[yh], lsem.at[4]),
        pltpu.make_async_copy(gain, gain_all.at[yh], lsem.at[5]),
        pltpu.make_async_copy(bias, bias_all.at[yh], lsem.at[6]),
    ]
    for copy in own:
        copy.start()

    w_own.wait()
    for k in (1, 2, 3):
        wfrom = lax.rem(y + 4 - k, 4)
        arrived(w_all.at[wfrom // 2, lax.rem(wfrom, 2), z, core], wr.at[k - 1])

    h_out, z_out = [], []

    def bundle(at):
        return w_all.at[:, :, at, core]

    def hand(at, slot):
        h_out.append(send(bundle(at), bundle(at), hs.at[slot], hr.at[slot], sibling))

    def pass_on(at, step):
        up, down = at
        if step < 3:
            z_out.append(send(bundle(up), bundle(up), zs.at[step], zr.at[step], z_dev(1)))
            z_out.append(send(bundle(down), bundle(down), zs.at[4 + step], zr.at[4 + step], z_dev(NZ - 1)))
        else:
            z_out.append(send(w_all.at[0, :, up, core], w_all.at[0, :, up, core], zs.at[3], zr.at[3], z_dev(1)))
            z_out.append(
                send(w_all.at[1, :, down, core], w_all.at[1, :, down, core], zs.at[7], zr.at[7], z_dev(NZ - 1))
            )

    def step_in(step):
        below, above = lax.rem(z + NZ - step, NZ), lax.rem(z + step, NZ)
        if step < 4:
            arrived(bundle(below), zr.at[step - 1])
            arrived(bundle(above), zr.at[4 + step - 1])
            pass_on((below, above), step)
            hand(below, 2 * step - 1)
            hand(above, 2 * step)
        else:
            arrived(w_all.at[0, :, below, core], zr.at[3])
            arrived(w_all.at[1, :, below, core], zr.at[7])
            hand(below, 7)

    def handed(step):
        below, above = lax.rem(z + NZ - step, NZ), lax.rem(z + step, NZ)
        if step == 0:
            arrived(w_all.at[:, :, z, 1 - core], hr.at[0])
        elif step < 4:
            arrived(w_all.at[:, :, below, 1 - core], hr.at[2 * step - 1])
            arrived(w_all.at[:, :, above, 1 - core], hr.at[2 * step])
        else:
            arrived(w_all.at[:, :, below, 1 - core], hr.at[7])

    def multiply(pair, first):
        @pl.loop(0, LOCAL_WIDTH // 256)
        def _(n):
            block, at = n // 5, lax.rem(n, 5)
            cols = pl.ds(pl.multiple_of(at * 256, 256), 256)
            total = None
            for low in (0, 1):
                feats = pl.ds(pl.multiple_of((low * 4 + pair) * PAIR, PAIR), PAIR)
                a = ctx_all[:, :, feats].reshape(NX * ROWS, PAIR)
                b = w_all[block, low, pl.ds(pair * 2, 2), :, :, cols].reshape(PAIR, 256)
                term = jnp.dot(a, b, preferred_element_type=F32)
                total = term if total is None else total + term
            if first:
                hid[block, :, cols] = total
            else:
                hid[block, :, cols] += total

    pass_on((z, z), 0)
    hand(z, 0)

    arrived(ctx_part(ctx_all.at[left], 0), cr.at[0])
    c_out.append(
        send(ctx_part(ctx_all.at[left], 0), ctx_part(ctx_all.at[left], 0), cs.at[4], cr.at[4], x_dev(1))
    )
    arrived(ctx_part(ctx_all.at[right], 1), cr.at[3])
    c_out.append(
        send(ctx_part(ctx_all.at[right], 1), ctx_part(ctx_all.at[right], 1), cs.at[5], cr.at[5], x_dev(3))
    )
    step_in(1)

    for way in (0, 1):
        for block in (0, 1):
            arrived(transit.at[way, block], rr.at[way * 2 + block])
        spot = res_in.at[left if way == 0 else right, :, pl.ds(way * HALF, HALF)]
        r_out.append(send(transit.at[way], spot, rs.at[8 + way], rr.at[8 + way], x_dev(1 if way == 0 else 3)))

    own[3].wait()
    own[4].wait()
    own[5].wait()
    arrived(head_all.at[1 - yh], nr.at[0])
    arrived(gain_all.at[1 - yh], nr.at[1])
    arrived(bias_all.at[1 - yh], nr.at[2])
    g_row = jnp.zeros((8, VOCAB), F32)
    for block in (0, 1):
        lhs = jnp.concatenate(
            [
                jnp.broadcast_to(gain_all[block], (4, NB)),
                jnp.broadcast_to(bias_all[block], (4, NB)),
            ],
            axis=0,
        )
        for _ in range(3):
            top = lhs.astype(BF16)
            g_row += jnp.dot(top, head_all[block], preferred_element_type=F32)
            lhs = lhs - top.astype(F32)
    g_own[...] = g_row
    g_out = [send(g_own, g_in.at[k], gs.at[k], gr.at[k], x_dev(k + 1)) for k in range(3)]

    step_in(2)

    own[0].wait()
    arrived(ctx_part(ctx_all.at[left], 1), cr.at[1])
    arrived(ctx_part(ctx_all.at[right], 0), cr.at[2])
    arrived(ctx_part(ctx_all.at[opposite], 0), cr.at[4])
    arrived(ctx_part(ctx_all.at[opposite], 1), cr.at[5])

    base = z // 2
    odd = lax.rem(z, 2)
    handed(0)
    handed(1)
    multiply(base, True)
    step_in(3)
    handed(2)
    multiply(lax.rem(base + 3 + 2 * odd, 4), False)
    handed(3)
    multiply(lax.rem(base + 1 + 2 * odd, 4), False)
    step_in(4)
    handed(4)
    multiply(lax.rem(base + 2, 4), False)

    own[1].wait()
    own[2].wait()
    for way in (0, 1):
        frm = left if way == 0 else right
        for block in (0, 1):
            arrived(res_in.at[frm, block], rr.at[4 + way * 2 + block])
    for way in (0, 1):
        arrived(res_in.at[opposite, :, pl.ds(way * HALF, HALF)], rr.at[8 + way])

    def block_part(k):
        rows_of = lax.rem(x + k + 1, NX)
        at = pl.ds(pl.multiple_of(rows_of * ROWS, ROWS), ROWS)
        row_sum = jnp.zeros((ROWS, 1), F32)
        for block in (0, 1):
            full = hid[block, at] + res_in[rows_of, block].astype(F32)
            hid[block, at] = full
            row_sum += jnp.sum(full, axis=1, keepdims=True)
        mean = row_sum * (1.0 / LOCAL_WIDTH)
        square = jnp.zeros((ROWS, 1), F32)
        product = jnp.zeros((ROWS, VOCAB), F32)
        for block in (0, 1):
            off = hid[block, at] - mean
            square += jnp.sum(off * off, axis=1, keepdims=True)
            scaled = off * gain_all[block]
            top = scaled.astype(BF16)
            rest = (scaled - top.astype(F32)).astype(BF16)
            product += jnp.dot(top, head_all[block], preferred_element_type=F32)
            product += jnp.dot(rest, head_all[block], preferred_element_type=F32)
        lane = lax.broadcasted_iota(jnp.int32, (ROWS, VOCAB), 1)
        part[k, :, :VOCAB] = product
        part[k, :, VOCAB:] = jnp.where(lane == 0, mean, square)

    @pl.loop(0, 3)
    def _(k):
        block_part(k)
        send(part.at[k], part_in.at[k], ps.at[k], pr.at[k], x_dev(k + 1))

    block_part(3)

    label = jnp.transpose(jnp.broadcast_to(info[0:1, :].astype(F32), (VOCAB, 256)))[:ROWS]
    for k in range(3):
        arrived(g_in.at[k], gr.at[k])
        arrived(part_in.at[k], pr.at[k])
    parts = [part[3]] + [part_in[k] for k in range(3)]
    sums = [g_own[...]] + [g_in[k] for k in range(3)]
    means = [p[:, VOCAB : VOCAB + 1] for p in parts]
    squares = [p[:, VOCAB + 1 : VOCAB + 2] for p in parts]
    center = (means[0] + means[1] + means[2] + means[3]) * 0.25
    total_square = squares[0] + squares[1] + squares[2] + squares[3]
    logits = jnp.zeros((ROWS, VOCAB), F32)
    shift = jnp.zeros((1, VOCAB), F32)
    for p, g, m in zip(parts, sums, means):
        away = m - center
        total_square += LOCAL_WIDTH * (away * away)
        logits += p[:, :VOCAB] + away * g[0:1]
        shift += g[4:5]
    logits = logits * lax.rsqrt(total_square * (1.0 / WIDTH) + EPS) + shift
    largest = jnp.max(logits, axis=1, keepdims=True)
    log_total = largest + jnp.log(jnp.sum(jnp.exp(logits - largest), axis=1, keepdims=True))
    token = lax.broadcasted_iota(jnp.int32, (ROWS, VOCAB), 1).astype(F32)
    picked = jnp.sum(jnp.where(token == label, logits, 0.0), axis=1, keepdims=True)
    score = jnp.broadcast_to(picked - log_total, (ROWS, VOCAB))
    score_rows = jnp.transpose(jnp.concatenate([score, jnp.zeros((256 - ROWS, VOCAB), F32)], axis=0))

    group = info[1:2, :]
    place = info[2:3, :]
    lhs = jnp.where(lax.broadcasted_iota(jnp.int32, (NDP, 256), 0) == group, score_rows[:NDP], 0.0)
    spots = jnp.where(lax.broadcasted_iota(jnp.int32, (VOCAB, 256), 0) == place, 1.0, 0.0).astype(BF16)
    packed = jnp.zeros((NDP, VOCAB), F32)
    for _ in range(3):
        top = lhs.astype(BF16)
        packed += lax.dot_general(top, spots, (((1,), (1,)), ((), ())), preferred_element_type=F32)
        lhs = lhs - top.astype(F32)
    dp_send[...] = packed.reshape(NDP, 1, VOCAB)

    @pl.loop(1, NDP)
    def _(k):
        to = lax.rem(dp + k, NDP)
        send(dp_send.at[to], dp_in.at[k - 1], ds_.at[0], dr.at[0], (to, tensor))

    live_score = jnp.where(group >= 0, score_rows[0:1], 0.0)
    res_out[...] = live_score[:, :ROWS]
    at_row = lax.broadcasted_iota(jnp.int32, (1, 256), 1)
    lane = lax.broadcasted_iota(jnp.int32, (1, VOCAB), 1)
    begin = jnp.int32(0)
    proteins = jnp.zeros((1, VOCAB), F32)
    for i in range(4):
        length = lens[i]
        end = begin + length
        inside = jnp.where((at_row >= begin) & (at_row < end), live_score, 0.0)
        one = jnp.sum(inside, axis=1, keepdims=True) / jnp.broadcast_to(
            jnp.maximum(length, 1).astype(F32), (1, 1)
        )
        proteins = jnp.where(lane == i, one, proteins)
        begin = end
    pr_out[...] = proteins[:, :4]

    for copy in w_out + c_out + r_out + n_out + z_out + h_out + g_out:
        copy.wait_send()
    for k in range(3):
        arrived(part.at[k], ps.at[k])
    arrived(dp_in, dr.at[0])
    arrived(dp_in, ds_.at[0])
    packed_row = dp_send[dp] + jnp.sum(dp_in[...], axis=0)
    pk_out[...] = packed_row[:, :HALF]


def shards(context, residual, out_weight, norm_gain, norm_bias, head_weight, targets, packing, lengths):
    info = jnp.pad(
        jnp.concatenate([targets[None], packing], axis=0), ((0, 5), (0, 256 - ROWS)), constant_values=-1
    )
    any_ = pl.BlockSpec(memory_space=pl.ANY)
    vmem = pl.BlockSpec(memory_space=pltpu.VMEM)
    dma = pltpu.SemaphoreType.DMA
    scores, packed, proteins = pl.pallas_call(
        kernel,
        out_shape=(
            jax.ShapeDtypeStruct((1, ROWS), F32),
            jax.ShapeDtypeStruct((1, HALF), F32),
            jax.ShapeDtypeStruct((1, 4), F32),
        ),
        in_specs=[any_] * 6 + [vmem, pl.BlockSpec(memory_space=pltpu.SMEM)],
        out_specs=(vmem, vmem, vmem),
        scratch_shapes=[
            pltpu.VMEM((NX, ROWS, CTX), BF16),
            pltpu.VMEM((NX, 2, ROWS, NB), BF16),
            pltpu.VMEM((2, 2, HALF, NB), BF16),
            pltpu.VMEM((2, 2, NZ, 2, KB, NB), BF16),
            pltpu.VMEM((2, NX * ROWS, NB), F32),
            pltpu.VMEM((2, NB, VOCAB), BF16),
            pltpu.VMEM((2, 1, NB), F32),
            pltpu.VMEM((2, 1, NB), F32),
            pltpu.VMEM((8, VOCAB), F32),
            pltpu.VMEM((3, 8, VOCAB), F32),
            pltpu.VMEM((4, ROWS, 2 * VOCAB), F32),
            pltpu.VMEM((3, ROWS, 2 * VOCAB), F32),
            pltpu.VMEM((NDP, 1, VOCAB), F32),
            pltpu.VMEM((NDP - 1, 1, VOCAB), F32),
            dma((7,)),
            dma((6,)), dma((6,)),
            dma((10,)), dma((10,)),
            dma((3,)), dma((3,)),
            dma((8,)), dma((8,)),
            dma((8,)), dma((8,)),
            dma((3,)), dma((3,)),
            dma((3,)), dma((3,)),
            dma((3,)), dma((3,)),
            dma((1,)), dma((1,)),
        ],
        compiler_params=pltpu.CompilerParams(
            collective_id=0, has_side_effects=True, vmem_limit_bytes=60 * 2**20
        ),
    )(
        context, residual, out_weight, head_weight,
        norm_gain.reshape(1, NB), norm_bias.reshape(1, NB), info, lengths,
    )
    return scores.reshape(ROWS), packed.reshape(HALF), proteins.reshape(4)


def solution(mesh):
    placed = (
        P(("dp", "tensor"), None),
        P(("dp", "tensor"), None),
        P("dp", "tensor"),
        P("tensor"),
        P("tensor"),
        P("tensor", None),
        P(("dp", "tensor")),
        P(None, ("dp", "tensor")),
        P(("dp", "tensor")),
    )
    rows = P(("dp", "tensor"))
    return jax.shard_map(shards, mesh=mesh, in_specs=placed, out_specs=(rows, rows, rows), check_vma=False)
```

```python
import jax
import jax.numpy as jnp
from jax import lax
from jax.experimental import pallas as pl
from jax.experimental.pallas import tpu as pltpu
from jax.sharding import PartitionSpec as P

MESH = pl.DeviceIdType.MESH
F32 = jnp.float32
BF16 = jnp.bfloat16
EPS = 1e-05
NX, NZ, NDP = 4, 8, 32
ROWS, HALF = 192, 96
KB, NB, CTX, VOCAB = 160, 1280, 5120, 128
LOCAL_WIDTH = 2 * NB
WIDTH = NX * LOCAL_WIDTH
RA = 64
RB = KB - RA
RH = RB // 2
PAIR = 4 * KB


def kernel(
    ctx, res, w, head, gain, bias, targets, packing, lens,
    out,
    ctx_all, res_in, transit, w_all, hid, head_all, gain_all, bias_all,
    g_own, g_in, part, part_in, info, dp_send, dp_in,
    lsem, cs, cr, rs, rr, ws, wr, zs, zr, bs, br, us, ur, os, or_, hs, hr, ns, nr, gs, gr, ps, pr, ds_, dr,
):
    dp = lax.axis_index("dp")
    tensor = lax.axis_index("tensor")
    core = lax.rem(dp, 2)
    z = lax.rem(dp // 2, NZ)
    yl = dp // (2 * NZ)
    x = lax.rem(tensor, NX)
    yh = tensor // NX
    y = yh * 2 + yl

    def x_dev(k):
        return (dp, yh * NX + lax.rem(x + k, NX))

    def y_dev(k):
        to = lax.rem(y + k, 4)
        return ((lax.rem(to, 2) * NZ + z) * 2 + core, (to // 2) * NX + x)

    def z_dev(k):
        return ((yl * NZ + lax.rem(z + k, NZ)) * 2 + core, tensor)

    sibling = (dp + 1 - 2 * core, tensor)
    left, right = lax.rem(x + 3, NX), lax.rem(x + 1, NX)

    def send(src, dst, ssem, rsem, dev):
        copy = pltpu.make_async_remote_copy(
            src_ref=src, dst_ref=dst, send_sem=ssem, recv_sem=rsem,
            device_id=dev, device_id_type=MESH,
        )
        copy.start()
        return copy

    def arrived(ref, sem):
        pltpu.make_async_copy(ref, ref, sem).wait()

    barrier = pltpu.get_barrier_semaphore()

    @pl.loop(1, NDP)
    def _(k):
        pl.semaphore_signal(barrier, inc=1, device_id=(lax.rem(dp + k, NDP), tensor), device_id_type=MESH)

    for k in (1, 2, 3):
        pl.semaphore_signal(barrier, inc=1, device_id=x_dev(k), device_id_type=MESH)
    for other in (yl, 1 - yl):
        pl.semaphore_signal(
            barrier, inc=1, device_id=((other * NZ + z) * 2 + core, (1 - yh) * NX + x), device_id_type=MESH
        )
    pl.semaphore_wait(barrier, NDP - 1 + 5)

    first, second = pl.ds(0, RA), pl.ds(RA, RB)
    upper, lower = pl.ds(RA, RH), pl.ds(RA + RH, RH)

    def piece(of_y, at, rows):
        return w_all.at[of_y // 2, lax.rem(of_y, 2), at, core, rows]

    b_out = []
    w_out = [send(w.at[first], piece(y, z, first), ws.at[k - 1], wr.at[k - 1], y_dev(k)) for k in (1, 2, 3)]
    for way, to in ((0, z_dev(1)), (1, z_dev(NZ - 1))):
        b_out.append(send(w.at[second], piece(y, z, second), bs.at[4 * way], br.at[4 * way], to))
    for way, to in ((0, y_dev(1)), (1, y_dev(3))):
        b_out.append(send(w.at[second], piece(y, z, second), us.at[way], ur.at[way], to))
    w_own = pltpu.make_async_copy(w, w_all.at[yh, yl, z, core], lsem.at[0])
    w_own.start()

    def ctx_part(ref, part_of):
        return ref.at[pl.ds(part_of * HALF, HALF)]

    c_out = []

    def send_ctx(way, part_of):
        at = way * 2 + part_of
        c_out.append(
            send(
                ctx_part(ctx, part_of), ctx_part(ctx_all.at[x], part_of), cs.at[at], cr.at[at],
                x_dev(1 if way == 0 else 3),
            )
        )

    def columns(block, to):
        return pl.ds(pl.multiple_of((block * NX + to) * NB, NB), NB)

    opposite = lax.rem(x + 2, NX)
    r_out = []
    send_ctx(0, 0)
    send_ctx(1, 1)
    for way in (0, 1):
        for block in (0, 1):
            at = way * 2 + block
            r_out.append(
                send(
                    res.at[pl.ds(way * HALF, HALF), columns(block, opposite)], transit.at[way, block],
                    rs.at[at], rr.at[at], x_dev(1 if way == 0 else 3),
                )
            )
    send_ctx(0, 1)
    send_ctx(1, 0)
    for way in (0, 1):
        for block in (0, 1):
            at = 4 + way * 2 + block
            r_out.append(
                send(
                    res.at[:, columns(block, right if way == 0 else left)], res_in.at[x, block],
                    rs.at[at], rr.at[at], x_dev(1 if way == 0 else 3),
                )
            )
    partner = y_dev(2)
    n_out = [
        send(head, head_all.at[yh], ns.at[0], nr.at[0], partner),
        send(gain, gain_all.at[yh, 0], ns.at[1], nr.at[1], partner),
        send(bias, bias_all.at[yh, 0], ns.at[2], nr.at[2], partner),
    ]
    own = [
        pltpu.make_async_copy(ctx, ctx_all.at[x], lsem.at[1]),
        pltpu.make_async_copy(res.at[:, columns(0, x)], res_in.at[x, 0], lsem.at[2]),
        pltpu.make_async_copy(res.at[:, columns(1, x)], res_in.at[x, 1], lsem.at[3]),
        pltpu.make_async_copy(head, head_all.at[yh], lsem.at[4]),
        pltpu.make_async_copy(gain, gain_all.at[yh, 0], lsem.at[5]),
        pltpu.make_async_copy(bias, bias_all.at[yh, 0], lsem.at[6]),
    ]
    for copy in own:
        copy.start()

    h_out, z_out = [], []

    def below(step):
        return lax.rem(z + NZ - step, NZ)

    def above(step):
        return lax.rem(z + step, NZ)

    def spots(step):
        if step == 0:
            return [(z, 0)]
        if step == 4:
            return [(below(4), 7)]
        return [(below(step), 2 * step - 1), (above(step), 2 * step)]

    def bundle(at):
        return w_all.at[:, :, at, core, first]

    def a_in(step):
        if step == 0:
            w_own.wait()
            for k in (1, 2, 3):
                arrived(piece(lax.rem(y + 4 - k, 4), z, first), wr.at[k - 1])
        elif step < 4:
            arrived(bundle(below(step)), zr.at[step - 1])
            arrived(bundle(above(step)), zr.at[4 + step - 1])
        else:
            arrived(w_all.at[0, :, below(4), core, first], zr.at[3])
            arrived(w_all.at[1, :, below(4), core, first], zr.at[7])
        if step < 3:
            up, down = bundle(below(step)), bundle(above(step))
        elif step == 3:
            up, down = w_all.at[0, :, below(3), core, first], w_all.at[1, :, above(3), core, first]
        else:
            return
        z_out.append(send(up, up, zs.at[step], zr.at[step], z_dev(1)))
        z_out.append(send(down, down, zs.at[4 + step], zr.at[4 + step], z_dev(NZ - 1)))

    def b_in(step):
        if step < 4:
            arrived(piece(y, below(step), second), br.at[step - 1])
            arrived(piece(y, above(step), second), br.at[4 + step - 1])
            up_rows, down_rows = (second, second) if step < 3 else (upper, lower)
            up, down = piece(y, below(step), up_rows), piece(y, above(step), down_rows)
            b_out.append(send(up, up, bs.at[step], br.at[step], z_dev(1)))
            b_out.append(send(down, down, bs.at[4 + step], br.at[4 + step], z_dev(NZ - 1)))
        else:
            arrived(piece(y, below(4), upper), br.at[3])
            arrived(piece(y, below(4), lower), br.at[7])
        for at, number in spots(step):
            spot = piece(y, at, second)
            b_out.append(send(spot, spot, us.at[2 * number], ur.at[2 * number], y_dev(1)))
            b_out.append(send(spot, spot, us.at[2 * number + 1], ur.at[2 * number + 1], y_dev(3)))

    def relay(step):
        for at, number in spots(step):
            for way, frm, rows in ((0, lax.rem(y + 3, 4), upper), (1, lax.rem(y + 1, 4), lower)):
                arrived(piece(frm, at, second), ur.at[2 * number + way])
                spot = piece(frm, at, rows)
                b_out.append(
                    send(spot, spot, os.at[2 * number + way], or_.at[2 * number + way], y_dev(1 if way == 0 else 3))
                )

    def hand(step):
        for at, number in spots(step):
            for way, rows in ((0, upper), (1, lower)):
                arrived(piece(lax.rem(y + 2, 4), at, rows), or_.at[2 * number + way])
            whole = w_all.at[:, :, at, core]
            h_out.append(send(whole, whole, hs.at[number], hr.at[number], sibling))

    def handed(step):
        for at, number in spots(step):
            arrived(w_all.at[:, :, at, 1 - core], hr.at[number])

    def multiply(pair, start):
        @pl.loop(0, LOCAL_WIDTH // 256)
        def _(n):
            block, at = n // 5, lax.rem(n, 5)
            cols = pl.ds(pl.multiple_of(at * 256, 256), 256)
            total = None
            for low in (0, 1):
                feats = pl.ds(pl.multiple_of((low * 4 + pair) * PAIR, PAIR), PAIR)
                a = ctx_all[:, :, feats].reshape(NX * ROWS, PAIR)
                b = w_all[block, low, pl.ds(pair * 2, 2), :, :, cols].reshape(PAIR, 256)
                term = jnp.dot(a, b, preferred_element_type=F32)
                total = term if total is None else total + term
            if start:
                hid[block, :, cols] = total
            else:
                hid[block, :, cols] += total

    a_in(0)
    b_in(1)
    relay(0)

    arrived(ctx_part(ctx_all.at[left], 0), cr.at[0])
    c_out.append(
        send(ctx_part(ctx_all.at[left], 0), ctx_part(ctx_all.at[left], 0), cs.at[4], cr.at[4], x_dev(1))
    )
    arrived(ctx_part(ctx_all.at[right], 1), cr.at[3])
    c_out.append(
        send(ctx_part(ctx_all.at[right], 1), ctx_part(ctx_all.at[right], 1), cs.at[5], cr.at[5], x_dev(3))
    )
    a_in(1)
    b_in(2)
    relay(1)
    hand(0)

    for way in (0, 1):
        for block in (0, 1):
            arrived(transit.at[way, block], rr.at[way * 2 + block])
        spot = res_in.at[left if way == 0 else right, :, pl.ds(way * HALF, HALF)]
        r_out.append(send(transit.at[way], spot, rs.at[8 + way], rr.at[8 + way], x_dev(1 if way == 0 else 3)))

    own[3].wait()
    own[4].wait()
    own[5].wait()
    arrived(head_all.at[1 - yh], nr.at[0])
    arrived(gain_all.at[1 - yh, 0], nr.at[1])
    arrived(bias_all.at[1 - yh, 0], nr.at[2])
    g_row = jnp.zeros((8, VOCAB), F32)
    for block in (0, 1):
        lhs = jnp.concatenate(
            [
                jnp.broadcast_to(gain_all[block], (4, NB)),
                jnp.broadcast_to(bias_all[block], (4, NB)),
            ],
            axis=0,
        )
        for _ in range(3):
            top = lhs.astype(BF16)
            g_row += jnp.dot(top, head_all[block], preferred_element_type=F32)
            lhs = lhs - top.astype(F32)
    g_own[...] = g_row
    g_out = [send(g_own, g_in.at[k], gs.at[k], gr.at[k], x_dev(k + 1)) for k in range(3)]

    a_in(2)
    b_in(3)
    relay(2)
    hand(1)

    own[0].wait()
    arrived(ctx_part(ctx_all.at[left], 1), cr.at[1])
    arrived(ctx_part(ctx_all.at[right], 0), cr.at[2])
    arrived(ctx_part(ctx_all.at[opposite], 0), cr.at[4])
    arrived(ctx_part(ctx_all.at[opposite], 1), cr.at[5])

    base = z // 2
    odd = lax.rem(z, 2)
    handed(0)
    handed(1)
    multiply(base, True)
    a_in(3)
    b_in(4)
    relay(3)
    hand(2)
    handed(2)
    multiply(lax.rem(base + 3 + 2 * odd, 4), False)
    a_in(4)
    relay(4)
    hand(3)
    handed(3)
    multiply(lax.rem(base + 1 + 2 * odd, 4), False)
    hand(4)
    handed(4)
    multiply(lax.rem(base + 2, 4), False)

    own[1].wait()
    own[2].wait()
    for way in (0, 1):
        frm = left if way == 0 else right
        for block in (0, 1):
            arrived(res_in.at[frm, block], rr.at[4 + way * 2 + block])
    for way in (0, 1):
        arrived(res_in.at[opposite, :, pl.ds(way * HALF, HALF)], rr.at[8 + way])

    def block_part(k):
        rows_of = lax.rem(x + k + 1, NX)
        at = pl.ds(pl.multiple_of(rows_of * ROWS, ROWS), ROWS)
        row_sum = jnp.zeros((ROWS, 1), F32)
        for block in (0, 1):
            full = hid[block, at] + res_in[rows_of, block].astype(F32)
            hid[block, at] = full
            row_sum += jnp.sum(full, axis=1, keepdims=True)
        mean = row_sum * (1.0 / LOCAL_WIDTH)
        square = jnp.zeros((ROWS, 1), F32)
        product = jnp.zeros((ROWS, VOCAB), F32)
        for block in (0, 1):
            off = hid[block, at] - mean
            square += jnp.sum(off * off, axis=1, keepdims=True)
            scaled = off * gain_all[block]
            top = scaled.astype(BF16)
            rest = (scaled - top.astype(F32)).astype(BF16)
            product += jnp.dot(top, head_all[block], preferred_element_type=F32)
            product += jnp.dot(rest, head_all[block], preferred_element_type=F32)
        lane = lax.broadcasted_iota(jnp.int32, (ROWS, VOCAB), 1)
        both = jnp.concatenate(
            [jnp.where(lane == 0, mean, square), jnp.zeros((256 - ROWS, VOCAB), F32)], axis=0
        )
        both = jnp.transpose(both)[:8]
        part[k, :ROWS] = product
        part[k, ROWS : ROWS + 8] = both[:, :VOCAB]
        part[k, ROWS + 8 :] = both[:, VOCAB:]

    @pl.loop(0, 3)
    def _(k):
        block_part(k)
        send(part.at[k], part_in.at[k], ps.at[k], pr.at[k], x_dev(k + 1))

    block_part(3)

    info[...] = jnp.full((8, 256), -1, jnp.int32)
    info[0:1, :ROWS] = targets[...].reshape(1, ROWS)
    info[1:3, :ROWS] = packing[...]
    label = jnp.transpose(jnp.broadcast_to(info[0:1, :].astype(F32), (VOCAB, 256)))[:ROWS]
    for k in range(3):
        arrived(g_in.at[k], gr.at[k])
        arrived(part_in.at[k], pr.at[k])
    parts = [part[3]] + [part_in[k] for k in range(3)]
    sums = [g_own[...]] + [g_in[k] for k in range(3)]
    stats = [jnp.concatenate([p[ROWS : ROWS + 8], p[ROWS + 8 :]], axis=1) for p in parts]
    center = (stats[0][0:1] + stats[1][0:1] + stats[2][0:1] + stats[3][0:1]) * 0.25
    total_square = stats[0][1:2] + stats[1][1:2] + stats[2][1:2] + stats[3][1:2]
    away = [st[0:1] - center for st in stats]
    for a in away:
        total_square += LOCAL_WIDTH * (a * a)
    inverse = lax.rsqrt(total_square * (1.0 / WIDTH) + EPS)
    by_row = jnp.transpose(jnp.concatenate([inverse, *away, jnp.zeros((VOCAB - 5, 256), F32)], axis=0))[:ROWS]
    logits = jnp.zeros((ROWS, VOCAB), F32)
    shift = jnp.zeros((1, VOCAB), F32)
    for i in range(4):
        logits += parts[i][:ROWS] + by_row[:, i + 1 : i + 2] * sums[i][0:1]
        shift += sums[i][4:5]
    logits = logits * by_row[:, 0:1] + shift
    largest = jnp.max(logits, axis=1, keepdims=True)
    log_total = largest + jnp.log(jnp.sum(jnp.exp(logits - largest), axis=1, keepdims=True))
    token = lax.broadcasted_iota(jnp.int32, (ROWS, VOCAB), 1).astype(F32)
    picked = jnp.sum(jnp.where(token == label, logits, 0.0), axis=1, keepdims=True)
    score = jnp.broadcast_to(picked - log_total, (ROWS, VOCAB))
    score_rows = jnp.transpose(jnp.concatenate([score, jnp.zeros((256 - ROWS, VOCAB), F32)], axis=0))

    group = info[1:2, :]
    place = info[2:3, :]
    lhs = jnp.where(lax.broadcasted_iota(jnp.int32, (NDP, 256), 0) == group, score_rows[:NDP], 0.0)
    chosen = jnp.where(lax.broadcasted_iota(jnp.int32, (VOCAB, 256), 0) == place, 1.0, 0.0).astype(BF16)
    packed = jnp.zeros((NDP, VOCAB), F32)
    for _ in range(3):
        top = lhs.astype(BF16)
        packed += lax.dot_general(top, chosen, (((1,), (1,)), ((), ())), preferred_element_type=F32)
        lhs = lhs - top.astype(F32)
    dp_send[...] = packed.reshape(NDP, 1, VOCAB)

    @pl.loop(1, NDP)
    def _(k):
        to = lax.rem(dp + k, NDP)
        send(dp_send.at[to], dp_in.at[k - 1], ds_.at[0], dr.at[0], (to, tensor))

    live_score = jnp.where(group >= 0, score_rows[0:1], 0.0)
    out[0:1] = live_score
    at_row = lax.broadcasted_iota(jnp.int32, (1, 256), 1)
    lane = lax.broadcasted_iota(jnp.int32, (1, VOCAB), 1)
    begin = jnp.int32(0)
    proteins = jnp.zeros((1, VOCAB), F32)
    for i in range(4):
        length = lens[i]
        end = begin + length
        inside = jnp.where((at_row >= begin) & (at_row < end), live_score, 0.0)
        one = jnp.sum(inside, axis=1, keepdims=True) / jnp.broadcast_to(
            jnp.maximum(length, 1).astype(F32), (1, 1)
        )
        proteins = jnp.where(lane == i, one, proteins)
        begin = end
    out[2:3, :VOCAB] = proteins

    for copy in w_out + c_out + r_out + n_out + z_out + b_out + h_out + g_out:
        copy.wait_send()
    for k in range(3):
        arrived(part.at[k], ps.at[k])
    arrived(dp_in, dr.at[0])
    arrived(dp_in, ds_.at[0])
    packed_row = dp_send[dp] + jnp.sum(dp_in[...], axis=0)
    out[1:2, :VOCAB] = packed_row


def shards(context, residual, out_weight, norm_gain, norm_bias, head_weight, targets, packing, lengths):
    any_ = pl.BlockSpec(memory_space=pl.ANY)
    vmem = pl.BlockSpec(memory_space=pltpu.VMEM)
    dma = pltpu.SemaphoreType.DMA
    rows = pl.pallas_call(
        kernel,
        out_shape=jax.ShapeDtypeStruct((8, 256), F32),
        in_specs=[any_] * 6 + [vmem, vmem, pl.BlockSpec(memory_space=pltpu.SMEM)],
        out_specs=vmem,
        scratch_shapes=[
            pltpu.VMEM((NX, ROWS, CTX), BF16),
            pltpu.VMEM((NX, 2, ROWS, NB), BF16),
            pltpu.VMEM((2, 2, HALF, NB), BF16),
            pltpu.VMEM((2, 2, NZ, 2, KB, NB), BF16),
            pltpu.VMEM((2, NX * ROWS, NB), F32),
            pltpu.VMEM((2, NB, VOCAB), BF16),
            pltpu.VMEM((2, 1, NB), F32),
            pltpu.VMEM((2, 1, NB), F32),
            pltpu.VMEM((8, VOCAB), F32),
            pltpu.VMEM((3, 8, VOCAB), F32),
            pltpu.VMEM((4, ROWS + 16, VOCAB), F32),
            pltpu.VMEM((3, ROWS + 16, VOCAB), F32),
            pltpu.VMEM((8, 256), jnp.int32),
            pltpu.VMEM((NDP, 1, VOCAB), F32),
            pltpu.VMEM((NDP - 1, 1, VOCAB), F32),
            dma((7,)),
            dma((6,)), dma((6,)),
            dma((10,)), dma((10,)),
            dma((3,)), dma((3,)),
            dma((8,)), dma((8,)),
            dma((8,)), dma((8,)),
            dma((16,)), dma((16,)),
            dma((16,)), dma((16,)),
            dma((8,)), dma((8,)),
            dma((3,)), dma((3,)),
            dma((3,)), dma((3,)),
            dma((3,)), dma((3,)),
            dma((1,)), dma((1,)),
        ],
        compiler_params=pltpu.CompilerParams(
            collective_id=0, has_side_effects=True, vmem_limit_bytes=60 * 2**20
        ),
    )(
        context, residual, out_weight, head_weight,
        norm_gain, norm_bias, targets, packing, lengths,
    )
    return rows[0, :ROWS], rows[1, :HALF], rows[2, :4]


def solution(mesh):
    placed = (
        P(("dp", "tensor"), None),
        P(("dp", "tensor"), None),
        P("dp", "tensor"),
        P("tensor"),
        P("tensor"),
        P("tensor", None),
        P(("dp", "tensor")),
        P(None, ("dp", "tensor")),
        P(("dp", "tensor")),
    )
    rows = P(("dp", "tensor"))
    return jax.shard_map(shards, mesh=mesh, in_specs=placed, out_specs=(rows, rows, rows), check_vma=False)
```

```python
import jax
import jax.numpy as jnp
from jax import lax
from jax.experimental import pallas as pl
from jax.experimental.pallas import tpu as pltpu
from jax.sharding import PartitionSpec as P

MESH = pl.DeviceIdType.MESH
F32 = jnp.float32
BF16 = jnp.bfloat16
EPS = 1e-05
NX, NZ, NDP = 4, 8, 32
ROWS, HALF = 192, 96
KB, NB, CTX, VOCAB = 160, 1280, 5120, 128
LOCAL_WIDTH = 2 * NB
WIDTH = NX * LOCAL_WIDTH
RA = 64
RB = KB - RA
RH = RB // 2
PAIR = 4 * KB


def kernel(
    ctx, res, w, head, gain, bias, targets, packing, lens,
    out,
    ctx_all, res_in, transit, w_all, hid, head_all, gain_all, bias_all,
    g_own, g_in, part, part_in, info, dp_send, dp_in,
    lsem, cs, cr, rs, rr, ws, wr, zs, zr, bs, br, us, ur, os, or_, hs, hr, ns, nr, gs, gr, ps, pr, ds_, dr,
):
    dp = lax.axis_index("dp")
    tensor = lax.axis_index("tensor")
    core = lax.rem(dp, 2)
    z = lax.rem(dp // 2, NZ)
    yl = dp // (2 * NZ)
    x = lax.rem(tensor, NX)
    yh = tensor // NX
    y = yh * 2 + yl

    def x_dev(k):
        return (dp, yh * NX + lax.rem(x + k, NX))

    def y_dev(k):
        to = lax.rem(y + k, 4)
        return ((lax.rem(to, 2) * NZ + z) * 2 + core, (to // 2) * NX + x)

    def z_dev(k):
        return ((yl * NZ + lax.rem(z + k, NZ)) * 2 + core, tensor)

    sibling = (dp + 1 - 2 * core, tensor)
    left, right = lax.rem(x + 3, NX), lax.rem(x + 1, NX)

    def send(src, dst, ssem, rsem, dev):
        copy = pltpu.make_async_remote_copy(
            src_ref=src, dst_ref=dst, send_sem=ssem, recv_sem=rsem,
            device_id=dev, device_id_type=MESH,
        )
        copy.start()
        return copy

    def arrived(ref, sem):
        pltpu.make_async_copy(ref, ref, sem).wait()

    barrier = pltpu.get_barrier_semaphore()
    for dev in [x_dev(k) for k in (1, 2, 3)] + [y_dev(k) for k in (1, 2, 3)] + [z_dev(1), z_dev(NZ - 1), sibling]:
        pl.semaphore_signal(barrier, inc=1, device_id=dev, device_id_type=MESH)
    pl.semaphore_wait(barrier, 9)

    first, second = pl.ds(0, RA), pl.ds(RA, RB)
    upper, lower = pl.ds(RA, RH), pl.ds(RA + RH, RH)

    def piece(of_y, at, rows):
        return w_all.at[of_y // 2, lax.rem(of_y, 2), at, core, rows]

    b_out = []
    w_out = [send(w.at[first], piece(y, z, first), ws.at[k - 1], wr.at[k - 1], y_dev(k)) for k in (1, 2, 3)]
    for way, to in ((0, z_dev(1)), (1, z_dev(NZ - 1))):
        b_out.append(send(w.at[second], piece(y, z, second), bs.at[4 * way], br.at[4 * way], to))
    for way, to in ((0, y_dev(1)), (1, y_dev(3))):
        b_out.append(send(w.at[second], piece(y, z, second), us.at[way], ur.at[way], to))
    w_own = pltpu.make_async_copy(w, w_all.at[yh, yl, z, core], lsem.at[0])
    w_own.start()

    def ctx_part(ref, part_of):
        return ref.at[pl.ds(part_of * HALF, HALF)]

    c_out = []

    def send_ctx(way, part_of):
        at = way * 2 + part_of
        c_out.append(
            send(
                ctx_part(ctx, part_of), ctx_part(ctx_all.at[x], part_of), cs.at[at], cr.at[at],
                x_dev(1 if way == 0 else 3),
            )
        )

    def columns(block, to):
        return pl.ds(pl.multiple_of((block * NX + to) * NB, NB), NB)

    opposite = lax.rem(x + 2, NX)
    r_out = []
    send_ctx(0, 0)
    send_ctx(1, 1)
    send_ctx(0, 1)
    send_ctx(1, 0)

    def res_far():
        for way in (0, 1):
            for block in (0, 1):
                at = way * 2 + block
                r_out.append(
                    send(
                        res.at[pl.ds(way * HALF, HALF), columns(block, opposite)], transit.at[way, block],
                        rs.at[at], rr.at[at], x_dev(1 if way == 0 else 3),
                    )
                )

    def res_near():
        for way in (0, 1):
            for block in (0, 1):
                at = 4 + way * 2 + block
                r_out.append(
                    send(
                        res.at[:, columns(block, right if way == 0 else left)], res_in.at[x, block],
                        rs.at[at], rr.at[at], x_dev(1 if way == 0 else 3),
                    )
                )

    def res_relay():
        for way in (0, 1):
            for block in (0, 1):
                arrived(transit.at[way, block], rr.at[way * 2 + block])
            spot = res_in.at[left if way == 0 else right, :, pl.ds(way * HALF, HALF)]
            r_out.append(send(transit.at[way], spot, rs.at[8 + way], rr.at[8 + way], x_dev(1 if way == 0 else 3)))

    partner = y_dev(2)
    n_out = [
        send(head, head_all.at[yh], ns.at[0], nr.at[0], partner),
        send(gain, gain_all.at[yh, 0], ns.at[1], nr.at[1], partner),
        send(bias, bias_all.at[yh, 0], ns.at[2], nr.at[2], partner),
    ]
    own = [
        pltpu.make_async_copy(ctx, ctx_all.at[x], lsem.at[1]),
        pltpu.make_async_copy(res.at[:, columns(0, x)], res_in.at[x, 0], lsem.at[2]),
        pltpu.make_async_copy(res.at[:, columns(1, x)], res_in.at[x, 1], lsem.at[3]),
        pltpu.make_async_copy(head, head_all.at[yh], lsem.at[4]),
        pltpu.make_async_copy(gain, gain_all.at[yh, 0], lsem.at[5]),
        pltpu.make_async_copy(bias, bias_all.at[yh, 0], lsem.at[6]),
    ]
    for copy in own:
        copy.start()

    h_out, z_out = [], []

    def below(step):
        return lax.rem(z + NZ - step, NZ)

    def above(step):
        return lax.rem(z + step, NZ)

    def spots(step):
        if step == 0:
            return [(z, 0)]
        if step == 4:
            return [(below(4), 7)]
        return [(below(step), 2 * step - 1), (above(step), 2 * step)]

    def bundle(at):
        return w_all.at[:, :, at, core, first]

    def a_in(step):
        if step == 0:
            w_own.wait()
            for k in (1, 2, 3):
                arrived(piece(lax.rem(y + 4 - k, 4), z, first), wr.at[k - 1])
        elif step < 4:
            arrived(bundle(below(step)), zr.at[step - 1])
            arrived(bundle(above(step)), zr.at[4 + step - 1])
        else:
            arrived(w_all.at[0, :, below(4), core, first], zr.at[3])
            arrived(w_all.at[1, :, below(4), core, first], zr.at[7])
        if step < 3:
            up, down = bundle(below(step)), bundle(above(step))
        elif step == 3:
            up, down = w_all.at[0, :, below(3), core, first], w_all.at[1, :, above(3), core, first]
        else:
            return
        z_out.append(send(up, up, zs.at[step], zr.at[step], z_dev(1)))
        z_out.append(send(down, down, zs.at[4 + step], zr.at[4 + step], z_dev(NZ - 1)))

    def b_in(step):
        if step < 4:
            arrived(piece(y, below(step), second), br.at[step - 1])
            arrived(piece(y, above(step), second), br.at[4 + step - 1])
            up_rows, down_rows = (second, second) if step < 3 else (upper, lower)
            up, down = piece(y, below(step), up_rows), piece(y, above(step), down_rows)
            b_out.append(send(up, up, bs.at[step], br.at[step], z_dev(1)))
            b_out.append(send(down, down, bs.at[4 + step], br.at[4 + step], z_dev(NZ - 1)))
        else:
            arrived(piece(y, below(4), upper), br.at[3])
            arrived(piece(y, below(4), lower), br.at[7])
        for at, number in spots(step):
            spot = piece(y, at, second)
            b_out.append(send(spot, spot, us.at[2 * number], ur.at[2 * number], y_dev(1)))
            b_out.append(send(spot, spot, us.at[2 * number + 1], ur.at[2 * number + 1], y_dev(3)))

    def relay(step):
        for at, number in spots(step):
            for way, frm, rows in ((0, lax.rem(y + 3, 4), upper), (1, lax.rem(y + 1, 4), lower)):
                arrived(piece(frm, at, second), ur.at[2 * number + way])
                spot = piece(frm, at, rows)
                b_out.append(
                    send(spot, spot, os.at[2 * number + way], or_.at[2 * number + way], y_dev(1 if way == 0 else 3))
                )

    def hand(step):
        for at, number in spots(step):
            for way, rows in ((0, upper), (1, lower)):
                arrived(piece(lax.rem(y + 2, 4), at, rows), or_.at[2 * number + way])
            whole = w_all.at[:, :, at, core]
            h_out.append(send(whole, whole, hs.at[number], hr.at[number], sibling))

    def handed(step):
        for at, number in spots(step):
            arrived(w_all.at[:, :, at, 1 - core], hr.at[number])

    def multiply(pair, start):
        @pl.loop(0, LOCAL_WIDTH // 256)
        def _(n):
            block, at = n // 5, lax.rem(n, 5)
            cols = pl.ds(pl.multiple_of(at * 256, 256), 256)
            a = jnp.concatenate(
                [
                    ctx_all[:, :, pl.ds(pl.multiple_of((low * 4 + pair) * PAIR, PAIR), PAIR)].reshape(NX * ROWS, PAIR)
                    for low in (0, 1)
                ],
                axis=1,
            )
            b = jnp.concatenate(
                [w_all[block, low, pl.ds(pair * 2, 2), :, :, cols].reshape(PAIR, 256) for low in (0, 1)], axis=0
            )
            total = jnp.dot(a, b, preferred_element_type=F32)
            if start:
                hid[block, :, cols] = total
            else:
                hid[block, :, cols] += total

    a_in(0)
    b_in(1)
    relay(0)

    a_in(1)
    b_in(2)

    arrived(ctx_part(ctx_all.at[left], 0), cr.at[0])
    c_out.append(
        send(ctx_part(ctx_all.at[left], 0), ctx_part(ctx_all.at[left], 0), cs.at[4], cr.at[4], x_dev(1))
    )
    arrived(ctx_part(ctx_all.at[right], 1), cr.at[3])
    c_out.append(
        send(ctx_part(ctx_all.at[right], 1), ctx_part(ctx_all.at[right], 1), cs.at[5], cr.at[5], x_dev(3))
    )
    relay(1)
    hand(0)

    own[3].wait()
    own[4].wait()
    own[5].wait()
    arrived(head_all.at[1 - yh], nr.at[0])
    arrived(gain_all.at[1 - yh, 0], nr.at[1])
    arrived(bias_all.at[1 - yh, 0], nr.at[2])
    g_row = jnp.zeros((8, VOCAB), F32)
    for block in (0, 1):
        lhs = jnp.concatenate(
            [
                jnp.broadcast_to(gain_all[block], (4, NB)),
                jnp.broadcast_to(bias_all[block], (4, NB)),
            ],
            axis=0,
        )
        for _ in range(3):
            top = lhs.astype(BF16)
            g_row += jnp.dot(top, head_all[block], preferred_element_type=F32)
            lhs = lhs - top.astype(F32)
    g_own[...] = g_row
    g_out = [send(g_own, g_in.at[k], gs.at[k], gr.at[k], x_dev(k + 1)) for k in range(3)]

    a_in(2)
    b_in(3)
    for copy in c_out[:4]:
        copy.wait_send()
    res_far()
    relay(2)
    hand(1)
    for copy in c_out[4:]:
        copy.wait_send()
    res_near()
    a_in(3)
    b_in(4)
    own[0].wait()
    arrived(ctx_part(ctx_all.at[left], 1), cr.at[1])
    arrived(ctx_part(ctx_all.at[right], 0), cr.at[2])
    arrived(ctx_part(ctx_all.at[opposite], 0), cr.at[4])
    arrived(ctx_part(ctx_all.at[opposite], 1), cr.at[5])
    relay(3)
    hand(2)

    base = z // 2
    odd = lax.rem(z, 2)
    handed(0)
    handed(1)
    multiply(base, True)
    res_relay()
    a_in(4)
    relay(4)
    hand(3)
    handed(2)
    multiply(lax.rem(base + 3 + 2 * odd, 4), False)
    hand(4)
    handed(3)
    multiply(lax.rem(base + 1 + 2 * odd, 4), False)
    handed(4)
    multiply(lax.rem(base + 2, 4), False)

    own[1].wait()
    own[2].wait()
    for way in (0, 1):
        frm = left if way == 0 else right
        for block in (0, 1):
            arrived(res_in.at[frm, block], rr.at[4 + way * 2 + block])
    for way in (0, 1):
        arrived(res_in.at[opposite, :, pl.ds(way * HALF, HALF)], rr.at[8 + way])

    def block_part(k):
        rows_of = lax.rem(x + k + 1, NX)
        at = pl.ds(pl.multiple_of(rows_of * ROWS, ROWS), ROWS)
        row_sum = jnp.zeros((ROWS, 1), F32)
        for block in (0, 1):
            full = hid[block, at] + res_in[rows_of, block].astype(F32)
            hid[block, at] = full
            row_sum += jnp.sum(full, axis=1, keepdims=True)
        mean = row_sum * (1.0 / LOCAL_WIDTH)
        square = jnp.zeros((ROWS, 1), F32)
        product = jnp.zeros((ROWS, VOCAB), F32)
        for block in (0, 1):
            off = hid[block, at] - mean
            square += jnp.sum(off * off, axis=1, keepdims=True)
            scaled = off * gain_all[block]
            top = scaled.astype(BF16)
            rest = (scaled - top.astype(F32)).astype(BF16)
            product += jnp.dot(top, head_all[block], preferred_element_type=F32)
            product += jnp.dot(rest, head_all[block], preferred_element_type=F32)
        lane = lax.broadcasted_iota(jnp.int32, (ROWS, VOCAB), 1)
        both = jnp.concatenate(
            [jnp.where(lane == 0, mean, square), jnp.zeros((256 - ROWS, VOCAB), F32)], axis=0
        )
        both = jnp.transpose(both)[:8]
        part[k, :ROWS] = product
        part[k, ROWS : ROWS + 8] = both[:, :VOCAB]
        part[k, ROWS + 8 :] = both[:, VOCAB:]

    @pl.loop(0, 3)
    def _(k):
        block_part(k)
        send(part.at[k], part_in.at[k], ps.at[k], pr.at[k], x_dev(k + 1))

    block_part(3)

    info[...] = jnp.full((8, 256), -1, jnp.int32)
    info[0:1, :ROWS] = targets[...].reshape(1, ROWS)
    info[1:3, :ROWS] = packing[...]
    label = jnp.transpose(jnp.broadcast_to(info[0:1, :].astype(F32), (VOCAB, 256)))[:ROWS]
    for k in range(3):
        arrived(g_in.at[k], gr.at[k])
        arrived(part_in.at[k], pr.at[k])
    parts = [part[3]] + [part_in[k] for k in range(3)]
    sums = [g_own[...]] + [g_in[k] for k in range(3)]
    stats = [jnp.concatenate([p[ROWS : ROWS + 8], p[ROWS + 8 :]], axis=1) for p in parts]
    center = (stats[0][0:1] + stats[1][0:1] + stats[2][0:1] + stats[3][0:1]) * 0.25
    total_square = stats[0][1:2] + stats[1][1:2] + stats[2][1:2] + stats[3][1:2]
    away = [st[0:1] - center for st in stats]
    for a in away:
        total_square += LOCAL_WIDTH * (a * a)
    inverse = lax.rsqrt(total_square * (1.0 / WIDTH) + EPS)
    by_row = jnp.transpose(jnp.concatenate([inverse, *away, jnp.zeros((VOCAB - 5, 256), F32)], axis=0))[:ROWS]
    logits = jnp.zeros((ROWS, VOCAB), F32)
    shift = jnp.zeros((1, VOCAB), F32)
    for i in range(4):
        logits += parts[i][:ROWS] + by_row[:, i + 1 : i + 2] * sums[i][0:1]
        shift += sums[i][4:5]
    logits = logits * by_row[:, 0:1] + shift
    largest = jnp.max(logits, axis=1, keepdims=True)
    log_total = largest + jnp.log(jnp.sum(jnp.exp(logits - largest), axis=1, keepdims=True))
    token = lax.broadcasted_iota(jnp.int32, (ROWS, VOCAB), 1).astype(F32)
    picked = jnp.sum(jnp.where(token == label, logits, 0.0), axis=1, keepdims=True)
    score = jnp.broadcast_to(picked - log_total, (ROWS, VOCAB))
    score_rows = jnp.transpose(jnp.concatenate([score, jnp.zeros((256 - ROWS, VOCAB), F32)], axis=0))

    group = info[1:2, :]
    place = info[2:3, :]
    lhs = jnp.where(lax.broadcasted_iota(jnp.int32, (NDP, 256), 0) == group, score_rows[:NDP], 0.0)
    chosen = jnp.where(lax.broadcasted_iota(jnp.int32, (VOCAB, 256), 0) == place, 1.0, 0.0).astype(BF16)
    packed = jnp.zeros((NDP, VOCAB), F32)
    for _ in range(3):
        top = lhs.astype(BF16)
        packed += lax.dot_general(top, chosen, (((1,), (1,)), ((), ())), preferred_element_type=F32)
        lhs = lhs - top.astype(F32)
    dp_send[...] = packed.reshape(NDP, 1, VOCAB)

    @pl.loop(1, NDP)
    def _(k):
        to = lax.rem(dp + k, NDP)
        send(dp_send.at[to], dp_in.at[k - 1], ds_.at[0], dr.at[0], (to, tensor))

    live_score = jnp.where(group >= 0, score_rows[0:1], 0.0)
    out[0:1] = live_score
    at_row = lax.broadcasted_iota(jnp.int32, (1, 256), 1)
    lane = lax.broadcasted_iota(jnp.int32, (1, VOCAB), 1)
    begin = jnp.int32(0)
    proteins = jnp.zeros((1, VOCAB), F32)
    for i in range(4):
        length = lens[i]
        end = begin + length
        inside = jnp.where((at_row >= begin) & (at_row < end), live_score, 0.0)
        one = jnp.sum(inside, axis=1, keepdims=True) / jnp.broadcast_to(
            jnp.maximum(length, 1).astype(F32), (1, 1)
        )
        proteins = jnp.where(lane == i, one, proteins)
        begin = end
    out[2:3, :VOCAB] = proteins

    for copy in w_out + r_out + n_out + z_out + b_out + h_out + g_out:
        copy.wait_send()
    for k in range(3):
        arrived(part.at[k], ps.at[k])
    arrived(dp_in, dr.at[0])
    arrived(dp_in, ds_.at[0])
    packed_row = dp_send[dp] + jnp.sum(dp_in[...], axis=0)
    out[1:2, :VOCAB] = packed_row


def deal(rows, scores, packed, proteins):
    scores[...] = rows[0:1, :ROWS].reshape(ROWS)
    packed[...] = rows[1:2, :HALF].reshape(HALF)
    proteins[...] = rows[2:3, :4].reshape(4)


def shards(context, residual, out_weight, norm_gain, norm_bias, head_weight, targets, packing, lengths):
    any_ = pl.BlockSpec(memory_space=pl.ANY)
    vmem = pl.BlockSpec(memory_space=pltpu.VMEM)
    dma = pltpu.SemaphoreType.DMA
    rows = pl.pallas_call(
        kernel,
        out_shape=jax.ShapeDtypeStruct((8, 256), F32),
        in_specs=[any_] * 6 + [vmem, vmem, pl.BlockSpec(memory_space=pltpu.SMEM)],
        out_specs=vmem,
        scratch_shapes=[
            pltpu.VMEM((NX, ROWS, CTX), BF16),
            pltpu.VMEM((NX, 2, ROWS, NB), BF16),
            pltpu.VMEM((2, 2, HALF, NB), BF16),
            pltpu.VMEM((2, 2, NZ, 2, KB, NB), BF16),
            pltpu.VMEM((2, NX * ROWS, NB), F32),
            pltpu.VMEM((2, NB, VOCAB), BF16),
            pltpu.VMEM((2, 1, NB), F32),
            pltpu.VMEM((2, 1, NB), F32),
            pltpu.VMEM((8, VOCAB), F32),
            pltpu.VMEM((3, 8, VOCAB), F32),
            pltpu.VMEM((4, ROWS + 16, VOCAB), F32),
            pltpu.VMEM((3, ROWS + 16, VOCAB), F32),
            pltpu.VMEM((8, 256), jnp.int32),
            pltpu.VMEM((NDP, 1, VOCAB), F32),
            pltpu.VMEM((NDP - 1, 1, VOCAB), F32),
            dma((7,)),
            dma((6,)), dma((6,)),
            dma((10,)), dma((10,)),
            dma((3,)), dma((3,)),
            dma((8,)), dma((8,)),
            dma((8,)), dma((8,)),
            dma((16,)), dma((16,)),
            dma((16,)), dma((16,)),
            dma((8,)), dma((8,)),
            dma((3,)), dma((3,)),
            dma((3,)), dma((3,)),
            dma((3,)), dma((3,)),
            dma((1,)), dma((1,)),
        ],
        compiler_params=pltpu.CompilerParams(
            collective_id=0, has_side_effects=True, vmem_limit_bytes=60 * 2**20
        ),
    )(
        context, residual, out_weight, head_weight,
        norm_gain, norm_bias, targets, packing, lengths,
    )
    return pl.pallas_call(
        deal,
        out_shape=tuple(jax.ShapeDtypeStruct((n,), F32) for n in (ROWS, HALF, 4)),
        in_specs=[vmem],
        out_specs=(vmem, vmem, vmem),
    )(rows)


def solution(mesh):
    placed = (
        P(("dp", "tensor"), None),
        P(("dp", "tensor"), None),
        P("dp", "tensor"),
        P("tensor"),
        P("tensor"),
        P("tensor", None),
        P(("dp", "tensor")),
        P(None, ("dp", "tensor")),
        P(("dp", "tensor")),
    )
    rows = P(("dp", "tensor"))
    return jax.shard_map(shards, mesh=mesh, in_specs=placed, out_specs=(rows, rows, rows), check_vma=False)
```

```python
import jax
import jax.numpy as jnp
from jax import lax
from jax.experimental import pallas as pl
from jax.experimental.pallas import tpu as pltpu
from jax.sharding import PartitionSpec as P

MESH = pl.DeviceIdType.MESH
F32 = jnp.float32
BF16 = jnp.bfloat16
EPS = 1e-05
NX, NZ, NDP = 4, 8, 32
ROWS, HALF = 192, 96
KB, NB, CTX, VOCAB = 160, 1280, 5120, 128
LOCAL_WIDTH = 2 * NB
WIDTH = NX * LOCAL_WIDTH
RA = 64
RB = KB - RA
RH = RB // 2
PAIR = 4 * KB


def kernel(
    ctx, res, w, head, gain, bias, targets, packing, lens,
    out,
    ctx_all, res_in, transit, w_all, hid, head_all, gain_all, bias_all,
    g_own, g_in, part, part_in, info, dp_send, dp_in,
    lsem, cs, cr, rs, rr, ws, wr, zs, zr, bs, br, us, ur, os, or_, hs, hr, ns, nr, gs, gr, ps, pr, ds_, dr,
):
    dp = lax.axis_index("dp")
    tensor = lax.axis_index("tensor")
    core = lax.rem(dp, 2)
    z = lax.rem(dp // 2, NZ)
    yl = dp // (2 * NZ)
    x = lax.rem(tensor, NX)
    yh = tensor // NX
    y = yh * 2 + yl

    def x_dev(k):
        return (dp, yh * NX + lax.rem(x + k, NX))

    def y_dev(k):
        to = lax.rem(y + k, 4)
        return ((lax.rem(to, 2) * NZ + z) * 2 + core, (to // 2) * NX + x)

    def z_dev(k):
        return ((yl * NZ + lax.rem(z + k, NZ)) * 2 + core, tensor)

    sibling = (dp + 1 - 2 * core, tensor)
    left, right = lax.rem(x + 3, NX), lax.rem(x + 1, NX)

    def send(src, dst, ssem, rsem, dev):
        copy = pltpu.make_async_remote_copy(
            src_ref=src, dst_ref=dst, send_sem=ssem, recv_sem=rsem,
            device_id=dev, device_id_type=MESH,
        )
        copy.start()
        return copy

    def arrived(ref, sem):
        pltpu.make_async_copy(ref, ref, sem).wait()

    barrier = pltpu.get_barrier_semaphore()
    for dev in [x_dev(k) for k in (1, 2, 3)] + [y_dev(k) for k in (1, 2, 3)] + [z_dev(1), z_dev(NZ - 1), sibling]:
        pl.semaphore_signal(barrier, inc=1, device_id=dev, device_id_type=MESH)
    pl.semaphore_wait(barrier, 9)

    first, second = pl.ds(0, RA), pl.ds(RA, RB)
    upper, lower = pl.ds(RA, RH), pl.ds(RA + RH, RH)

    def piece(of_y, at, rows):
        return w_all.at[of_y // 2, lax.rem(of_y, 2), at, core, rows]

    def ctx_part(ref, part_of):
        return ref.at[pl.ds(part_of * HALF, HALF)]

    c_out = []

    def send_ctx(way, part_of):
        at = way * 2 + part_of
        c_out.append(
            send(
                ctx_part(ctx, part_of), ctx_part(ctx_all.at[x], part_of), cs.at[at], cr.at[at],
                x_dev(1 if way == 0 else 3),
            )
        )

    def columns(block, to):
        return pl.ds(pl.multiple_of((block * NX + to) * NB, NB), NB)

    opposite = lax.rem(x + 2, NX)
    r_out = []
    send_ctx(0, 0)
    send_ctx(1, 1)
    send_ctx(0, 1)
    send_ctx(1, 0)

    b_out = []
    w_out = [send(w.at[first], piece(y, z, first), ws.at[k - 1], wr.at[k - 1], y_dev(k)) for k in (1, 2, 3)]
    for way, to in ((0, z_dev(1)), (1, z_dev(NZ - 1))):
        b_out.append(send(w.at[second], piece(y, z, second), bs.at[4 * way], br.at[4 * way], to))
    for way, to in ((0, y_dev(1)), (1, y_dev(3))):
        b_out.append(send(w.at[second], piece(y, z, second), us.at[way], ur.at[way], to))
    w_own = pltpu.make_async_copy(w, w_all.at[yh, yl, z, core], lsem.at[0])
    w_own.start()


    def res_far():
        for way in (0, 1):
            for block in (0, 1):
                at = way * 2 + block
                r_out.append(
                    send(
                        res.at[pl.ds(way * HALF, HALF), columns(block, opposite)], transit.at[way, block],
                        rs.at[at], rr.at[at], x_dev(1 if way == 0 else 3),
                    )
                )

    def res_near(half):
        rows = pl.ds(half * HALF, HALF)
        for way in (0, 1):
            for block in (0, 1):
                at = 4 + 4 * half + 2 * way + block
                r_out.append(
                    send(
                        res.at[rows, columns(block, right if way == 0 else left)], res_in.at[x, block, rows],
                        rs.at[at], rr.at[at], x_dev(1 if way == 0 else 3),
                    )
                )

    def res_relay():
        for way in (0, 1):
            for block in (0, 1):
                at = way * 2 + block
                arrived(transit.at[way, block], rr.at[at])
                spot = res_in.at[left if way == 0 else right, block, pl.ds(way * HALF, HALF)]
                r_out.append(
                    send(transit.at[way, block], spot, rs.at[12 + at], rr.at[12 + at], x_dev(1 if way == 0 else 3))
                )

    partner = y_dev(2)
    n_out = [
        send(head, head_all.at[yh], ns.at[0], nr.at[0], partner),
        send(gain, gain_all.at[yh, 0], ns.at[1], nr.at[1], partner),
        send(bias, bias_all.at[yh, 0], ns.at[2], nr.at[2], partner),
    ]
    own = [
        pltpu.make_async_copy(ctx, ctx_all.at[x], lsem.at[1]),
        pltpu.make_async_copy(res.at[:, columns(0, x)], res_in.at[x, 0], lsem.at[2]),
        pltpu.make_async_copy(res.at[:, columns(1, x)], res_in.at[x, 1], lsem.at[3]),
        pltpu.make_async_copy(head, head_all.at[yh], lsem.at[4]),
        pltpu.make_async_copy(gain, gain_all.at[yh, 0], lsem.at[5]),
        pltpu.make_async_copy(bias, bias_all.at[yh, 0], lsem.at[6]),
    ]
    for copy in own:
        copy.start()

    h_out, z_out = [], []

    def below(step):
        return lax.rem(z + NZ - step, NZ)

    def above(step):
        return lax.rem(z + step, NZ)

    def spots(step):
        if step == 0:
            return [(z, 0)]
        if step == 4:
            return [(below(4), 7)]
        return [(below(step), 2 * step - 1), (above(step), 2 * step)]

    def bundle(at):
        return w_all.at[:, :, at, core, first]

    def a_in(step):
        if step == 0:
            w_own.wait()
            for k in (1, 2, 3):
                arrived(piece(lax.rem(y + 4 - k, 4), z, first), wr.at[k - 1])
        elif step < 4:
            arrived(bundle(below(step)), zr.at[step - 1])
            arrived(bundle(above(step)), zr.at[4 + step - 1])
        else:
            arrived(w_all.at[0, :, below(4), core, first], zr.at[3])
            arrived(w_all.at[1, :, below(4), core, first], zr.at[7])
        if step < 3:
            up, down = bundle(below(step)), bundle(above(step))
        elif step == 3:
            up, down = w_all.at[0, :, below(3), core, first], w_all.at[1, :, above(3), core, first]
        else:
            return
        z_out.append(send(up, up, zs.at[step], zr.at[step], z_dev(1)))
        z_out.append(send(down, down, zs.at[4 + step], zr.at[4 + step], z_dev(NZ - 1)))

    def b_in(step):
        if step < 4:
            arrived(piece(y, below(step), second), br.at[step - 1])
            arrived(piece(y, above(step), second), br.at[4 + step - 1])
            up_rows, down_rows = (second, second) if step < 3 else (upper, lower)
            up, down = piece(y, below(step), up_rows), piece(y, above(step), down_rows)
            b_out.append(send(up, up, bs.at[step], br.at[step], z_dev(1)))
            b_out.append(send(down, down, bs.at[4 + step], br.at[4 + step], z_dev(NZ - 1)))
        else:
            arrived(piece(y, below(4), upper), br.at[3])
            arrived(piece(y, below(4), lower), br.at[7])
        for at, number in spots(step):
            spot = piece(y, at, second)
            b_out.append(send(spot, spot, us.at[2 * number], ur.at[2 * number], y_dev(1)))
            b_out.append(send(spot, spot, us.at[2 * number + 1], ur.at[2 * number + 1], y_dev(3)))

    def relay(step):
        for at, number in spots(step):
            for way, frm, rows in ((0, lax.rem(y + 3, 4), upper), (1, lax.rem(y + 1, 4), lower)):
                arrived(piece(frm, at, second), ur.at[2 * number + way])
                spot = piece(frm, at, rows)
                b_out.append(
                    send(spot, spot, os.at[2 * number + way], or_.at[2 * number + way], y_dev(1 if way == 0 else 3))
                )

    def hand(step):
        for at, number in spots(step):
            for way, rows in ((0, upper), (1, lower)):
                arrived(piece(lax.rem(y + 2, 4), at, rows), or_.at[2 * number + way])
            whole = w_all.at[:, :, at, core]
            h_out.append(send(whole, whole, hs.at[number], hr.at[number], sibling))

    def handed(step):
        for at, number in spots(step):
            arrived(w_all.at[:, :, at, 1 - core], hr.at[number])

    def multiply(pair, start):
        @pl.loop(0, LOCAL_WIDTH // 256)
        def _(n):
            block, at = n // 5, lax.rem(n, 5)
            cols = pl.ds(pl.multiple_of(at * 256, 256), 256)
            a = jnp.concatenate(
                [
                    ctx_all[:, :, pl.ds(pl.multiple_of((low * 4 + pair) * PAIR, PAIR), PAIR)].reshape(NX * ROWS, PAIR)
                    for low in (0, 1)
                ],
                axis=1,
            )
            b = jnp.concatenate(
                [w_all[block, low, pl.ds(pair * 2, 2), :, :, cols].reshape(PAIR, 256) for low in (0, 1)], axis=0
            )
            total = jnp.dot(a, b, preferred_element_type=F32)
            if start:
                hid[block, :, cols] = total
            else:
                hid[block, :, cols] += total

    a_in(0)
    b_in(1)
    relay(0)

    a_in(1)
    b_in(2)

    arrived(ctx_part(ctx_all.at[left], 0), cr.at[0])
    c_out.append(
        send(ctx_part(ctx_all.at[left], 0), ctx_part(ctx_all.at[left], 0), cs.at[4], cr.at[4], x_dev(1))
    )
    arrived(ctx_part(ctx_all.at[right], 1), cr.at[3])
    c_out.append(
        send(ctx_part(ctx_all.at[right], 1), ctx_part(ctx_all.at[right], 1), cs.at[5], cr.at[5], x_dev(3))
    )
    relay(1)
    hand(0)

    own[3].wait()
    own[4].wait()
    own[5].wait()
    arrived(head_all.at[1 - yh], nr.at[0])
    arrived(gain_all.at[1 - yh, 0], nr.at[1])
    arrived(bias_all.at[1 - yh, 0], nr.at[2])
    g_row = jnp.zeros((8, VOCAB), F32)
    for block in (0, 1):
        lhs = jnp.concatenate(
            [
                jnp.broadcast_to(gain_all[block], (4, NB)),
                jnp.broadcast_to(bias_all[block], (4, NB)),
            ],
            axis=0,
        )
        for _ in range(3):
            top = lhs.astype(BF16)
            g_row += jnp.dot(top, head_all[block], preferred_element_type=F32)
            lhs = lhs - top.astype(F32)
    g_own[...] = g_row
    g_out = [send(g_own, g_in.at[k], gs.at[k], gr.at[k], x_dev(k + 1)) for k in range(3)]

    a_in(2)
    b_in(3)
    for copy in c_out[:4]:
        copy.wait_send()
    res_far()
    relay(2)
    hand(1)
    for copy in c_out[4:]:
        copy.wait_send()
    res_near(0)
    a_in(3)
    b_in(4)
    own[0].wait()
    arrived(ctx_part(ctx_all.at[left], 1), cr.at[1])
    arrived(ctx_part(ctx_all.at[right], 0), cr.at[2])
    arrived(ctx_part(ctx_all.at[opposite], 0), cr.at[4])
    arrived(ctx_part(ctx_all.at[opposite], 1), cr.at[5])
    relay(3)
    hand(2)

    base = z // 2
    odd = lax.rem(z, 2)
    handed(0)
    handed(1)
    multiply(base, True)
    res_relay()
    a_in(4)
    relay(4)
    hand(3)
    handed(2)
    multiply(lax.rem(base + 3 + 2 * odd, 4), False)
    res_near(1)
    hand(4)
    handed(3)
    multiply(lax.rem(base + 1 + 2 * odd, 4), False)
    handed(4)
    multiply(lax.rem(base + 2, 4), False)

    def half_block(k, half):
        rows_of = lax.rem(x + k + 1, NX)
        at = pl.ds(pl.multiple_of(rows_of * ROWS + half * HALF, HALF), HALF)
        within = pl.ds(half * HALF, HALF)
        row_sum = jnp.zeros((HALF, 1), F32)
        for block in (0, 1):
            full = hid[block, at] + res_in[rows_of, block, within].astype(F32)
            hid[block, at] = full
            row_sum += jnp.sum(full, axis=1, keepdims=True)
        mean = row_sum * (1.0 / LOCAL_WIDTH)
        square = jnp.zeros((HALF, 1), F32)
        product = jnp.zeros((2 * HALF, VOCAB), F32)
        for block in (0, 1):
            off = hid[block, at] - mean
            square += jnp.sum(off * off, axis=1, keepdims=True)
            scaled = off * gain_all[block]
            top = scaled.astype(BF16)
            rest = (scaled - top.astype(F32)).astype(BF16)
            product += jnp.dot(
                jnp.concatenate([top, rest], axis=0), head_all[block], preferred_element_type=F32
            )
        lane = lax.broadcasted_iota(jnp.int32, (HALF, VOCAB), 1)
        both = jnp.concatenate(
            [jnp.where(lane == 0, mean, square), jnp.zeros((VOCAB - HALF, VOCAB), F32)], axis=0
        )
        part[k, half, :HALF] = product[:HALF] + product[HALF:]
        part[k, half, HALF:] = jnp.transpose(both)[:8]
        if k < 3:
            p_out.append(
                send(part.at[k, half], part_in.at[k, half], ps.at[2 * k + half], pr.at[2 * k + half], x_dev(k + 1))
            )

    p_out = []
    own[1].wait()
    own[2].wait()
    for half in (0, 1):
        half_block(3, half)
    for copy in w_out + n_out + z_out + b_out + h_out + g_out:
        copy.wait_send()
    for half in (0, 1):
        for block in (0, 1):
            arrived(res_in.at[opposite, block, pl.ds(half * HALF, HALF)], rr.at[12 + 2 * half + block])
        half_block(1, half)
    for half in (0, 1):
        for way in (0, 1):
            for block in (0, 1):
                arrived(
                    res_in.at[left if way == 0 else right, block, pl.ds(half * HALF, HALF)],
                    rr.at[4 + 4 * half + 2 * way + block],
                )
            half_block(2 if way == 0 else 0, half)

    info[...] = jnp.full((8, 256), -1, jnp.int32)
    info[0:1, :ROWS] = targets[...].reshape(1, ROWS)
    info[1:3, :ROWS] = packing[...]
    label = jnp.transpose(jnp.broadcast_to(info[0:1, :].astype(F32), (VOCAB, 256)))[:ROWS]
    for k in range(3):
        arrived(g_in.at[k], gr.at[k])
        for half in (0, 1):
            arrived(part_in.at[k, half], pr.at[2 * k + half])
    parts = [part[3]] + [part_in[k] for k in range(3)]
    sums = [g_own[...]] + [g_in[k] for k in range(3)]
    stats = [jnp.concatenate([p[0, HALF:], p[1, HALF:]], axis=1) for p in parts]
    center = (stats[0][0:1] + stats[1][0:1] + stats[2][0:1] + stats[3][0:1]) * 0.25
    total_square = stats[0][1:2] + stats[1][1:2] + stats[2][1:2] + stats[3][1:2]
    away = [st[0:1] - center for st in stats]
    for a in away:
        total_square += LOCAL_WIDTH * (a * a)
    inverse = lax.rsqrt(total_square * (1.0 / WIDTH) + EPS)
    by_row = jnp.transpose(jnp.concatenate([inverse, *away, jnp.zeros((VOCAB - 5, 256), F32)], axis=0))
    by_row = jnp.concatenate([by_row[:HALF], by_row[VOCAB : VOCAB + HALF]], axis=0)
    logits = jnp.zeros((ROWS, VOCAB), F32)
    shift = jnp.zeros((1, VOCAB), F32)
    for i in range(4):
        logits += parts[i][:, :HALF].reshape(ROWS, VOCAB) + by_row[:, i + 1 : i + 2] * sums[i][0:1]
        shift += sums[i][4:5]
    logits = logits * by_row[:, 0:1] + shift
    largest = jnp.max(logits, axis=1, keepdims=True)
    log_total = largest + jnp.log(jnp.sum(jnp.exp(logits - largest), axis=1, keepdims=True))
    token = lax.broadcasted_iota(jnp.int32, (ROWS, VOCAB), 1).astype(F32)
    picked = jnp.sum(jnp.where(token == label, logits, 0.0), axis=1, keepdims=True)
    score = jnp.broadcast_to(picked - log_total, (ROWS, VOCAB))
    score_rows = jnp.transpose(jnp.concatenate([score, jnp.zeros((256 - ROWS, VOCAB), F32)], axis=0))

    group = info[1:2, :]
    place = info[2:3, :]
    lhs = jnp.where(lax.broadcasted_iota(jnp.int32, (NDP, 256), 0) == group, score_rows[:NDP], 0.0)
    chosen = jnp.where(lax.broadcasted_iota(jnp.int32, (VOCAB, 256), 0) == place, 1.0, 0.0).astype(BF16)
    packed = jnp.zeros((NDP, VOCAB), F32)
    for _ in range(3):
        top = lhs.astype(BF16)
        packed += lax.dot_general(top, chosen, (((1,), (1,)), ((), ())), preferred_element_type=F32)
        lhs = lhs - top.astype(F32)
    dp_send[...] = packed.reshape(NDP, 1, VOCAB)

    def deliver(k):
        to = lax.rem(dp + k, NDP)
        send(dp_send.at[to], dp_in.at[k - 1], ds_.at[0], dr.at[0], (to, tensor))

    pl.loop(8, NDP)(deliver)
    pl.loop(1, 8)(deliver)

    live_score = jnp.where(group >= 0, score_rows[0:1], 0.0)
    out[0:1] = live_score
    at_row = lax.broadcasted_iota(jnp.int32, (1, 256), 1)
    lane = lax.broadcasted_iota(jnp.int32, (1, VOCAB), 1)
    begin = jnp.int32(0)
    proteins = jnp.zeros((1, VOCAB), F32)
    for i in range(4):
        length = lens[i]
        end = begin + length
        inside = jnp.where((at_row >= begin) & (at_row < end), live_score, 0.0)
        one = jnp.sum(inside, axis=1, keepdims=True) / jnp.broadcast_to(
            jnp.maximum(length, 1).astype(F32), (1, 1)
        )
        proteins = jnp.where(lane == i, one, proteins)
        begin = end
    out[2:3, :VOCAB] = proteins

    for copy in r_out + p_out:
        copy.wait_send()
    arrived(dp_in, dr.at[0])
    arrived(dp_in, ds_.at[0])
    packed_row = dp_send[dp] + jnp.sum(dp_in[...], axis=0)
    out[1:2, :VOCAB] = packed_row


def deal(rows, scores, packed, proteins):
    scores[...] = rows[0:1, :ROWS].reshape(ROWS)
    packed[...] = rows[1:2, :HALF].reshape(HALF)
    proteins[...] = rows[2:3, :4].reshape(4)


def shards(context, residual, out_weight, norm_gain, norm_bias, head_weight, targets, packing, lengths):
    any_ = pl.BlockSpec(memory_space=pl.ANY)
    vmem = pl.BlockSpec(memory_space=pltpu.VMEM)
    dma = pltpu.SemaphoreType.DMA
    rows = pl.pallas_call(
        kernel,
        out_shape=jax.ShapeDtypeStruct((8, 256), F32),
        in_specs=[any_] * 6 + [vmem, vmem, pl.BlockSpec(memory_space=pltpu.SMEM)],
        out_specs=vmem,
        scratch_shapes=[
            pltpu.VMEM((NX, ROWS, CTX), BF16),
            pltpu.VMEM((NX, 2, ROWS, NB), BF16),
            pltpu.VMEM((2, 2, HALF, NB), BF16),
            pltpu.VMEM((2, 2, NZ, 2, KB, NB), BF16),
            pltpu.VMEM((2, NX * ROWS, NB), F32),
            pltpu.VMEM((2, NB, VOCAB), BF16),
            pltpu.VMEM((2, 1, NB), F32),
            pltpu.VMEM((2, 1, NB), F32),
            pltpu.VMEM((8, VOCAB), F32),
            pltpu.VMEM((3, 8, VOCAB), F32),
            pltpu.VMEM((4, 2, HALF + 8, VOCAB), F32),
            pltpu.VMEM((3, 2, HALF + 8, VOCAB), F32),
            pltpu.VMEM((8, 256), jnp.int32),
            pltpu.VMEM((NDP, 1, VOCAB), F32),
            pltpu.VMEM((NDP - 1, 1, VOCAB), F32),
            dma((7,)),
            dma((6,)), dma((6,)),
            dma((16,)), dma((16,)),
            dma((3,)), dma((3,)),
            dma((8,)), dma((8,)),
            dma((8,)), dma((8,)),
            dma((16,)), dma((16,)),
            dma((16,)), dma((16,)),
            dma((8,)), dma((8,)),
            dma((3,)), dma((3,)),
            dma((3,)), dma((3,)),
            dma((6,)), dma((6,)),
            dma((1,)), dma((1,)),
        ],
        compiler_params=pltpu.CompilerParams(
            collective_id=0, has_side_effects=True, vmem_limit_bytes=60 * 2**20
        ),
    )(
        context, residual, out_weight, head_weight,
        norm_gain, norm_bias, targets, packing, lengths,
    )
    return pl.pallas_call(
        deal,
        out_shape=tuple(jax.ShapeDtypeStruct((n,), F32) for n in (ROWS, HALF, 4)),
        in_specs=[vmem],
        out_specs=(vmem, vmem, vmem),
    )(rows)


def solution(mesh):
    placed = (
        P(("dp", "tensor"), None),
        P(("dp", "tensor"), None),
        P("dp", "tensor"),
        P("tensor"),
        P("tensor"),
        P("tensor", None),
        P(("dp", "tensor")),
        P(None, ("dp", "tensor")),
        P(("dp", "tensor")),
    )
    rows = P(("dp", "tensor"))
    return jax.shard_map(shards, mesh=mesh, in_specs=placed, out_specs=(rows, rows, rows), check_vma=False)
```

```python
import jax
import jax.numpy as jnp
from jax import lax
from jax.experimental import pallas as pl
from jax.experimental.pallas import tpu as pltpu
from jax.sharding import PartitionSpec as P

MESH = pl.DeviceIdType.MESH
F32 = jnp.float32
BF16 = jnp.bfloat16
EPS = 1e-05
NX, NZ, NDP = 4, 8, 32
ROWS, HALF = 192, 96
KB, NB, CTX, VOCAB = 160, 1280, 5120, 128
LOCAL_WIDTH = 2 * NB
WIDTH = NX * LOCAL_WIDTH
RA = 64
RB = KB - RA
RH = RB // 2
PAIR = 4 * KB


def kernel(
    ctx, res, w, head, gain, bias, targets_in, packing_in, lens_in,
    out,
    ctx_all, res_in, transit, w_all, hid, head_all, gain_all, bias_all,
    g_own, g_in, part, part_in, info, targets, packing, lens, dp_send, dp_in,
    lsem, cs, cr, rs, rr, ws, wr, zs, zr, bs, br, us, ur, os, or_, hs, hr, ns, nr, gs, gr, ps, pr, ds_, dr,
):
    dp = lax.axis_index("dp")
    tensor = lax.axis_index("tensor")
    core = lax.rem(dp, 2)
    z = lax.rem(dp // 2, NZ)
    yl = dp // (2 * NZ)
    x = lax.rem(tensor, NX)
    yh = tensor // NX
    y = yh * 2 + yl

    def x_dev(k):
        return (dp, yh * NX + lax.rem(x + k, NX))

    def y_dev(k):
        to = lax.rem(y + k, 4)
        return ((lax.rem(to, 2) * NZ + z) * 2 + core, (to // 2) * NX + x)

    def z_dev(k):
        return ((yl * NZ + lax.rem(z + k, NZ)) * 2 + core, tensor)

    sibling = (dp + 1 - 2 * core, tensor)
    left, right = lax.rem(x + 3, NX), lax.rem(x + 1, NX)

    def send(src, dst, ssem, rsem, dev):
        copy = pltpu.make_async_remote_copy(
            src_ref=src, dst_ref=dst, send_sem=ssem, recv_sem=rsem,
            device_id=dev, device_id_type=MESH,
        )
        copy.start()
        return copy

    def arrived(ref, sem):
        pltpu.make_async_copy(ref, ref, sem).wait()

    barrier = pltpu.get_barrier_semaphore()
    for dev in [x_dev(k) for k in (1, 2, 3)] + [y_dev(k) for k in (1, 2, 3)] + [z_dev(1), z_dev(NZ - 1), sibling]:
        pl.semaphore_signal(barrier, inc=1, device_id=dev, device_id_type=MESH)
    pl.semaphore_wait(barrier, 9)

    first, second = pl.ds(0, RA), pl.ds(RA, RB)
    upper, lower = pl.ds(RA, RH), pl.ds(RA + RH, RH)

    def piece(of_y, at, rows):
        return w_all.at[of_y // 2, lax.rem(of_y, 2), at, core, rows]

    def ctx_part(ref, part_of):
        return ref.at[pl.ds(part_of * HALF, HALF)]

    c_out = []

    def send_ctx(way, part_of):
        at = way * 2 + part_of
        c_out.append(
            send(
                ctx_part(ctx, part_of), ctx_part(ctx_all.at[x], part_of), cs.at[at], cr.at[at],
                x_dev(1 if way == 0 else 3),
            )
        )

    def columns(block, to):
        return pl.ds(pl.multiple_of((block * NX + to) * NB, NB), NB)

    opposite = lax.rem(x + 2, NX)
    r_out = []
    send_ctx(0, 0)
    send_ctx(1, 1)
    send_ctx(0, 1)
    send_ctx(1, 0)

    b_out = []
    w_out = [send(w.at[first], piece(y, z, first), ws.at[k - 1], wr.at[k - 1], y_dev(k)) for k in (1, 2, 3)]
    for way, to in ((0, z_dev(1)), (1, z_dev(NZ - 1))):
        b_out.append(send(w.at[second], piece(y, z, second), bs.at[4 * way], br.at[4 * way], to))
    for way, to in ((0, y_dev(1)), (1, y_dev(3))):
        b_out.append(send(w.at[second], piece(y, z, second), us.at[way], ur.at[way], to))
    w_own = pltpu.make_async_copy(w, w_all.at[yh, yl, z, core], lsem.at[0])
    w_own.start()


    def res_far():
        for way in (0, 1):
            for block in (0, 1):
                at = way * 2 + block
                r_out.append(
                    send(
                        res.at[pl.ds(way * HALF, HALF), columns(block, opposite)], transit.at[way, block],
                        rs.at[at], rr.at[at], x_dev(1 if way == 0 else 3),
                    )
                )

    def res_near(half):
        rows = pl.ds(half * HALF, HALF)
        for way in (0, 1):
            for block in (0, 1):
                at = 4 + 4 * half + 2 * way + block
                r_out.append(
                    send(
                        res.at[rows, columns(block, right if way == 0 else left)], res_in.at[x, block, rows],
                        rs.at[at], rr.at[at], x_dev(1 if way == 0 else 3),
                    )
                )

    def res_relay():
        for way in (0, 1):
            for block in (0, 1):
                at = way * 2 + block
                arrived(transit.at[way, block], rr.at[at])
                spot = res_in.at[left if way == 0 else right, block, pl.ds(way * HALF, HALF)]
                r_out.append(
                    send(transit.at[way, block], spot, rs.at[12 + at], rr.at[12 + at], x_dev(1 if way == 0 else 3))
                )

    partner = y_dev(2)
    n_out = [
        send(head, head_all.at[yh], ns.at[0], nr.at[0], partner),
        send(gain, gain_all.at[yh, 0], ns.at[1], nr.at[1], partner),
        send(bias, bias_all.at[yh, 0], ns.at[2], nr.at[2], partner),
    ]
    own = [
        pltpu.make_async_copy(ctx, ctx_all.at[x], lsem.at[1]),
        pltpu.make_async_copy(res.at[:, columns(0, x)], res_in.at[x, 0], lsem.at[2]),
        pltpu.make_async_copy(res.at[:, columns(1, x)], res_in.at[x, 1], lsem.at[3]),
        pltpu.make_async_copy(head, head_all.at[yh], lsem.at[4]),
        pltpu.make_async_copy(gain, gain_all.at[yh, 0], lsem.at[5]),
        pltpu.make_async_copy(bias, bias_all.at[yh, 0], lsem.at[6]),
        pltpu.make_async_copy(targets_in, targets, lsem.at[7]),
        pltpu.make_async_copy(packing_in, packing, lsem.at[8]),
        pltpu.make_async_copy(lens_in, lens, lsem.at[9]),
    ]
    for copy in own:
        copy.start()

    h_out, z_out = [], []

    def below(step):
        return lax.rem(z + NZ - step, NZ)

    def above(step):
        return lax.rem(z + step, NZ)

    def spots(step):
        if step == 0:
            return [(z, 0)]
        if step == 4:
            return [(below(4), 7)]
        return [(below(step), 2 * step - 1), (above(step), 2 * step)]

    def bundle(at):
        return w_all.at[:, :, at, core, first]

    def a_in(step):
        if step == 0:
            w_own.wait()
            for k in (1, 2, 3):
                arrived(piece(lax.rem(y + 4 - k, 4), z, first), wr.at[k - 1])
        elif step < 4:
            arrived(bundle(below(step)), zr.at[step - 1])
            arrived(bundle(above(step)), zr.at[4 + step - 1])
        else:
            arrived(w_all.at[0, :, below(4), core, first], zr.at[3])
            arrived(w_all.at[1, :, below(4), core, first], zr.at[7])
        if step < 3:
            up, down = bundle(below(step)), bundle(above(step))
        elif step == 3:
            up, down = w_all.at[0, :, below(3), core, first], w_all.at[1, :, above(3), core, first]
        else:
            return
        z_out.append(send(up, up, zs.at[step], zr.at[step], z_dev(1)))
        z_out.append(send(down, down, zs.at[4 + step], zr.at[4 + step], z_dev(NZ - 1)))

    def b_in(step):
        if step < 4:
            arrived(piece(y, below(step), second), br.at[step - 1])
            arrived(piece(y, above(step), second), br.at[4 + step - 1])
            up_rows, down_rows = (second, second) if step < 3 else (upper, lower)
            up, down = piece(y, below(step), up_rows), piece(y, above(step), down_rows)
            b_out.append(send(up, up, bs.at[step], br.at[step], z_dev(1)))
            b_out.append(send(down, down, bs.at[4 + step], br.at[4 + step], z_dev(NZ - 1)))
        else:
            arrived(piece(y, below(4), upper), br.at[3])
            arrived(piece(y, below(4), lower), br.at[7])
        for at, number in spots(step):
            spot = piece(y, at, second)
            b_out.append(send(spot, spot, us.at[2 * number], ur.at[2 * number], y_dev(1)))
            b_out.append(send(spot, spot, us.at[2 * number + 1], ur.at[2 * number + 1], y_dev(3)))

    def relay(step):
        for at, number in spots(step):
            for way, frm, rows in ((0, lax.rem(y + 3, 4), upper), (1, lax.rem(y + 1, 4), lower)):
                arrived(piece(frm, at, second), ur.at[2 * number + way])
                spot = piece(frm, at, rows)
                b_out.append(
                    send(spot, spot, os.at[2 * number + way], or_.at[2 * number + way], y_dev(1 if way == 0 else 3))
                )

    def hand(step):
        for at, number in spots(step):
            for way, rows in ((0, upper), (1, lower)):
                arrived(piece(lax.rem(y + 2, 4), at, rows), or_.at[2 * number + way])
            whole = w_all.at[:, :, at, core]
            h_out.append(send(whole, whole, hs.at[number], hr.at[number], sibling))

    def handed(step):
        for at, number in spots(step):
            arrived(w_all.at[:, :, at, 1 - core], hr.at[number])

    def multiply(pair, start):
        @pl.loop(0, LOCAL_WIDTH // 256)
        def _(n):
            block, at = n // 5, lax.rem(n, 5)
            cols = pl.ds(pl.multiple_of(at * 256, 256), 256)
            a = jnp.concatenate(
                [
                    ctx_all[:, :, pl.ds(pl.multiple_of((low * 4 + pair) * PAIR, PAIR), PAIR)].reshape(NX * ROWS, PAIR)
                    for low in (0, 1)
                ],
                axis=1,
            )
            b = jnp.concatenate(
                [w_all[block, low, pl.ds(pair * 2, 2), :, :, cols].reshape(PAIR, 256) for low in (0, 1)], axis=0
            )
            total = jnp.dot(a, b, preferred_element_type=F32)
            if start:
                hid[block, :, cols] = total
            else:
                hid[block, :, cols] += total

    a_in(0)
    b_in(1)
    relay(0)

    a_in(1)
    b_in(2)

    arrived(ctx_part(ctx_all.at[left], 0), cr.at[0])
    c_out.append(
        send(ctx_part(ctx_all.at[left], 0), ctx_part(ctx_all.at[left], 0), cs.at[4], cr.at[4], x_dev(1))
    )
    arrived(ctx_part(ctx_all.at[right], 1), cr.at[3])
    c_out.append(
        send(ctx_part(ctx_all.at[right], 1), ctx_part(ctx_all.at[right], 1), cs.at[5], cr.at[5], x_dev(3))
    )
    relay(1)
    hand(0)

    own[3].wait()
    own[4].wait()
    own[5].wait()
    arrived(head_all.at[1 - yh], nr.at[0])
    arrived(gain_all.at[1 - yh, 0], nr.at[1])
    arrived(bias_all.at[1 - yh, 0], nr.at[2])
    g_row = jnp.zeros((8, VOCAB), F32)
    for block in (0, 1):
        lhs = jnp.concatenate(
            [
                jnp.broadcast_to(gain_all[block], (4, NB)),
                jnp.broadcast_to(bias_all[block], (4, NB)),
            ],
            axis=0,
        )
        for _ in range(3):
            top = lhs.astype(BF16)
            g_row += jnp.dot(top, head_all[block], preferred_element_type=F32)
            lhs = lhs - top.astype(F32)
    g_own[...] = g_row
    g_out = [send(g_own, g_in.at[k], gs.at[k], gr.at[k], x_dev(k + 1)) for k in range(3)]

    a_in(2)
    b_in(3)
    for copy in c_out[:4]:
        copy.wait_send()
    res_far()
    relay(2)
    hand(1)
    for copy in c_out[4:]:
        copy.wait_send()
    res_near(0)
    a_in(3)
    b_in(4)
    own[0].wait()
    arrived(ctx_part(ctx_all.at[left], 1), cr.at[1])
    arrived(ctx_part(ctx_all.at[right], 0), cr.at[2])
    arrived(ctx_part(ctx_all.at[opposite], 0), cr.at[4])
    arrived(ctx_part(ctx_all.at[opposite], 1), cr.at[5])
    relay(3)
    hand(2)

    base = z // 2
    odd = lax.rem(z, 2)
    handed(0)
    handed(1)
    multiply(base, True)
    res_relay()
    a_in(4)
    relay(4)
    hand(3)
    handed(2)
    multiply(lax.rem(base + 3 + 2 * odd, 4), False)
    res_near(1)
    hand(4)
    handed(3)
    multiply(lax.rem(base + 1 + 2 * odd, 4), False)
    handed(4)
    multiply(lax.rem(base + 2, 4), False)

    def half_block(k, half):
        rows_of = lax.rem(x + k + 1, NX)
        at = pl.ds(pl.multiple_of(rows_of * ROWS + half * HALF, HALF), HALF)
        within = pl.ds(half * HALF, HALF)
        row_sum = jnp.zeros((HALF, 1), F32)
        for block in (0, 1):
            full = hid[block, at] + res_in[rows_of, block, within].astype(F32)
            hid[block, at] = full
            row_sum += jnp.sum(full, axis=1, keepdims=True)
        mean = row_sum * (1.0 / LOCAL_WIDTH)
        square = jnp.zeros((HALF, 1), F32)
        product = jnp.zeros((2 * HALF, VOCAB), F32)
        for block in (0, 1):
            off = hid[block, at] - mean
            square += jnp.sum(off * off, axis=1, keepdims=True)
            scaled = off * gain_all[block]
            top = scaled.astype(BF16)
            rest = (scaled - top.astype(F32)).astype(BF16)
            product += jnp.dot(
                jnp.concatenate([top, rest], axis=0), head_all[block], preferred_element_type=F32
            )
        lane = lax.broadcasted_iota(jnp.int32, (HALF, VOCAB), 1)
        both = jnp.concatenate(
            [jnp.where(lane == 0, mean, square), jnp.zeros((VOCAB - HALF, VOCAB), F32)], axis=0
        )
        part[k, half, :HALF] = product[:HALF] + product[HALF:]
        part[k, half, HALF:] = jnp.transpose(both)[:8]
        if k < 3:
            p_out.append(
                send(part.at[k, half], part_in.at[k, half], ps.at[2 * k + half], pr.at[2 * k + half], x_dev(k + 1))
            )

    p_out = []
    for copy in own[1:3] + own[6:]:
        copy.wait()
    for half in (0, 1):
        half_block(3, half)
    for copy in w_out + n_out + z_out + b_out + h_out + g_out:
        copy.wait_send()
    for half in (0, 1):
        for block in (0, 1):
            arrived(res_in.at[opposite, block, pl.ds(half * HALF, HALF)], rr.at[12 + 2 * half + block])
        half_block(1, half)
    for half in (0, 1):
        for way in (0, 1):
            for block in (0, 1):
                arrived(
                    res_in.at[left if way == 0 else right, block, pl.ds(half * HALF, HALF)],
                    rr.at[4 + 4 * half + 2 * way + block],
                )
            half_block(2 if way == 0 else 0, half)

    info[...] = jnp.full((8, 256), -1, jnp.int32)
    info[0:1, :ROWS] = targets[...].reshape(1, ROWS)
    info[1:3, :ROWS] = packing[...]
    label = jnp.transpose(jnp.broadcast_to(info[0:1, :].astype(F32), (VOCAB, 256)))[:ROWS]
    group = info[1:2, :]
    place = info[2:3, :]
    chosen = jnp.where(lax.broadcasted_iota(jnp.int32, (VOCAB, 256), 0) == place, 1.0, 0.0).astype(BF16)
    to_group = lax.broadcasted_iota(jnp.int32, (NDP, 256), 0) == group
    for k in range(3):
        arrived(g_in.at[k], gr.at[k])
        for half in (0, 1):
            arrived(part_in.at[k, half], pr.at[2 * k + half])
    parts = [part[3]] + [part_in[k] for k in range(3)]
    sums = [g_own[...]] + [g_in[k] for k in range(3)]
    stats = [jnp.concatenate([p[0, HALF:], p[1, HALF:]], axis=1) for p in parts]
    center = (stats[0][0:1] + stats[1][0:1] + stats[2][0:1] + stats[3][0:1]) * 0.25
    total_square = stats[0][1:2] + stats[1][1:2] + stats[2][1:2] + stats[3][1:2]
    away = [st[0:1] - center for st in stats]
    for a in away:
        total_square += LOCAL_WIDTH * (a * a)
    inverse = lax.rsqrt(total_square * (1.0 / WIDTH) + EPS)
    by_row = jnp.transpose(jnp.concatenate([inverse, *away, jnp.zeros((VOCAB - 5, 256), F32)], axis=0))
    by_row = jnp.concatenate([by_row[:HALF], by_row[VOCAB : VOCAB + HALF]], axis=0)
    logits = jnp.zeros((ROWS, VOCAB), F32)
    shift = jnp.zeros((1, VOCAB), F32)
    for i in range(4):
        logits += parts[i][:, :HALF].reshape(ROWS, VOCAB) + by_row[:, i + 1 : i + 2] * sums[i][0:1]
        shift += sums[i][4:5]
    logits = logits * by_row[:, 0:1] + shift
    largest = jnp.max(logits, axis=1, keepdims=True)
    log_total = largest + jnp.log(jnp.sum(jnp.exp(logits - largest), axis=1, keepdims=True))
    token = lax.broadcasted_iota(jnp.int32, (ROWS, VOCAB), 1).astype(F32)
    picked = jnp.sum(jnp.where(token == label, logits, 0.0), axis=1, keepdims=True)
    score = jnp.broadcast_to(picked - log_total, (ROWS, VOCAB))
    score_rows = jnp.transpose(jnp.concatenate([score, jnp.zeros((256 - ROWS, VOCAB), F32)], axis=0))

    lhs = jnp.where(to_group, score_rows[:NDP], 0.0)
    packed = jnp.zeros((NDP, VOCAB), F32)
    for _ in range(3):
        top = lhs.astype(BF16)
        packed += lax.dot_general(top, chosen, (((1,), (1,)), ((), ())), preferred_element_type=F32)
        lhs = lhs - top.astype(F32)
    dp_send[...] = packed.reshape(NDP, 1, VOCAB)

    def deliver(k):
        to = lax.rem(dp + k, NDP)
        send(dp_send.at[to], dp_in.at[k - 1], ds_.at[0], dr.at[0], (to, tensor))

    pl.loop(8, NDP)(deliver)
    pl.loop(1, 8)(deliver)

    live_score = jnp.where(group >= 0, score_rows[0:1], 0.0)
    out[0:1] = live_score
    at_row = lax.broadcasted_iota(jnp.int32, (1, 256), 1)
    lane = lax.broadcasted_iota(jnp.int32, (1, VOCAB), 1)
    begin = jnp.int32(0)
    proteins = jnp.zeros((1, VOCAB), F32)
    for i in range(4):
        length = lens[i]
        end = begin + length
        inside = jnp.where((at_row >= begin) & (at_row < end), live_score, 0.0)
        one = jnp.sum(inside, axis=1, keepdims=True) / jnp.broadcast_to(
            jnp.maximum(length, 1).astype(F32), (1, 1)
        )
        proteins = jnp.where(lane == i, one, proteins)
        begin = end
    out[2:3, :VOCAB] = proteins

    for copy in r_out + p_out:
        copy.wait_send()
    arrived(dp_in, dr.at[0])
    arrived(dp_in, ds_.at[0])
    packed_row = dp_send[dp] + jnp.sum(dp_in[...], axis=0)
    out[1:2, :VOCAB] = packed_row


def deal(rows, scores, packed, proteins):
    scores[...] = rows[0:1, :ROWS].reshape(ROWS)
    packed[...] = rows[1:2, :HALF].reshape(HALF)
    proteins[...] = rows[2:3, :4].reshape(4)


def shards(context, residual, out_weight, norm_gain, norm_bias, head_weight, targets, packing, lengths):
    any_ = pl.BlockSpec(memory_space=pl.ANY)
    vmem = pl.BlockSpec(memory_space=pltpu.VMEM)
    dma = pltpu.SemaphoreType.DMA
    rows = pl.pallas_call(
        kernel,
        out_shape=jax.ShapeDtypeStruct((8, 256), F32),
        in_specs=[any_] * 9,
        out_specs=vmem,
        scratch_shapes=[
            pltpu.VMEM((NX, ROWS, CTX), BF16),
            pltpu.VMEM((NX, 2, ROWS, NB), BF16),
            pltpu.VMEM((2, 2, HALF, NB), BF16),
            pltpu.VMEM((2, 2, NZ, 2, KB, NB), BF16),
            pltpu.VMEM((2, NX * ROWS, NB), F32),
            pltpu.VMEM((2, NB, VOCAB), BF16),
            pltpu.VMEM((2, 1, NB), F32),
            pltpu.VMEM((2, 1, NB), F32),
            pltpu.VMEM((8, VOCAB), F32),
            pltpu.VMEM((3, 8, VOCAB), F32),
            pltpu.VMEM((4, 2, HALF + 8, VOCAB), F32),
            pltpu.VMEM((3, 2, HALF + 8, VOCAB), F32),
            pltpu.VMEM((8, 256), jnp.int32),
            pltpu.VMEM((ROWS,), jnp.int32),
            pltpu.VMEM((2, ROWS), jnp.int32),
            pltpu.SMEM((4,), jnp.int32),
            pltpu.VMEM((NDP, 1, VOCAB), F32),
            pltpu.VMEM((NDP - 1, 1, VOCAB), F32),
            dma((10,)),
            dma((6,)), dma((6,)),
            dma((16,)), dma((16,)),
            dma((3,)), dma((3,)),
            dma((8,)), dma((8,)),
            dma((8,)), dma((8,)),
            dma((16,)), dma((16,)),
            dma((16,)), dma((16,)),
            dma((8,)), dma((8,)),
            dma((3,)), dma((3,)),
            dma((3,)), dma((3,)),
            dma((6,)), dma((6,)),
            dma((1,)), dma((1,)),
        ],
        compiler_params=pltpu.CompilerParams(
            collective_id=0, has_side_effects=True, vmem_limit_bytes=60 * 2**20
        ),
    )(
        context, residual, out_weight, head_weight,
        norm_gain, norm_bias, targets, packing, lengths,
    )
    return pl.pallas_call(
        deal,
        out_shape=tuple(jax.ShapeDtypeStruct((n,), F32) for n in (ROWS, HALF, 4)),
        in_specs=[vmem],
        out_specs=(vmem, vmem, vmem),
    )(rows)


def solution(mesh):
    placed = (
        P(("dp", "tensor"), None),
        P(("dp", "tensor"), None),
        P("dp", "tensor"),
        P("tensor"),
        P("tensor"),
        P("tensor", None),
        P(("dp", "tensor")),
        P(None, ("dp", "tensor")),
        P(("dp", "tensor")),
    )
    rows = P(("dp", "tensor"))
    return jax.shard_map(shards, mesh=mesh, in_specs=placed, out_specs=(rows, rows, rows), check_vma=False)
```

```python
import jax
import jax.numpy as jnp
from jax import lax
from jax.experimental import pallas as pl
from jax.experimental.pallas import tpu as pltpu
from jax.sharding import PartitionSpec as P

MESH = pl.DeviceIdType.MESH
F32 = jnp.float32
BF16 = jnp.bfloat16
EPS = 1e-05
NX, NZ, NDP = 4, 8, 32
ROWS, HALF = 192, 96
KB, NB, CTX, VOCAB = 160, 1280, 5120, 128
LOCAL_WIDTH = 2 * NB
WIDTH = NX * LOCAL_WIDTH
RA = 64
RB = KB - RA
RH = RB // 2
PAIR = 4 * KB


def kernel(
    ctx, res, w, head, gain, bias, targets_in, packing_in, lens_in,
    out,
    ctx_all, res_in, transit, w_all, hid, head_all, gain_all, bias_all,
    g_own, g_in, part, part_in, info, targets, packing, lens, dp_send, dp_in,
    lsem, cs, cr, rs, rr, ws, wr, zs, zr, bs, br, us, ur, os, or_, hs, hr, ns, nr, gs, gr, ps, pr, ds_, dr,
):
    dp = lax.axis_index("dp")
    tensor = lax.axis_index("tensor")
    core = lax.rem(dp, 2)
    z = lax.rem(dp // 2, NZ)
    yl = dp // (2 * NZ)
    x = lax.rem(tensor, NX)
    yh = tensor // NX
    y = yh * 2 + yl

    def x_dev(k):
        return (dp, yh * NX + lax.rem(x + k, NX))

    def y_dev(k):
        to = lax.rem(y + k, 4)
        return ((lax.rem(to, 2) * NZ + z) * 2 + core, (to // 2) * NX + x)

    def z_dev(k):
        return ((yl * NZ + lax.rem(z + k, NZ)) * 2 + core, tensor)

    sibling = (dp + 1 - 2 * core, tensor)
    left, right = lax.rem(x + 3, NX), lax.rem(x + 1, NX)

    def send(src, dst, ssem, rsem, dev):
        copy = pltpu.make_async_remote_copy(
            src_ref=src, dst_ref=dst, send_sem=ssem, recv_sem=rsem,
            device_id=dev, device_id_type=MESH,
        )
        copy.start()
        return copy

    def arrived(ref, sem):
        pltpu.make_async_copy(ref, ref, sem).wait()

    barrier = pltpu.get_barrier_semaphore()
    for dev in [x_dev(k) for k in (1, 2, 3)] + [y_dev(k) for k in (1, 2, 3)] + [z_dev(1), z_dev(NZ - 1), sibling]:
        pl.semaphore_signal(barrier, inc=1, device_id=dev, device_id_type=MESH)
    pl.semaphore_wait(barrier, 9)

    first, second = pl.ds(0, RA), pl.ds(RA, RB)
    upper, lower = pl.ds(RA, RH), pl.ds(RA + RH, RH)

    def piece(of_y, at, rows):
        return w_all.at[of_y // 2, lax.rem(of_y, 2), at, core, rows]

    def ctx_part(ref, part_of):
        return ref.at[pl.ds(part_of * HALF, HALF)]

    c_out = []

    def send_ctx(way, part_of):
        at = way * 2 + part_of
        c_out.append(
            send(
                ctx_part(ctx, part_of), ctx_part(ctx_all.at[x], part_of), cs.at[at], cr.at[at],
                x_dev(1 if way == 0 else 3),
            )
        )

    def columns(block, to):
        return pl.ds(pl.multiple_of((block * NX + to) * NB, NB), NB)

    opposite = lax.rem(x + 2, NX)
    r_out = []
    send_ctx(0, 0)
    send_ctx(1, 1)
    send_ctx(0, 1)
    send_ctx(1, 0)

    b_out = []
    w_out = [send(w.at[first], piece(y, z, first), ws.at[k - 1], wr.at[k - 1], y_dev(k)) for k in (1, 2, 3)]
    for way, to in ((0, z_dev(1)), (1, z_dev(NZ - 1))):
        b_out.append(send(w.at[second], piece(y, z, second), bs.at[4 * way], br.at[4 * way], to))
    for way, to in ((0, y_dev(1)), (1, y_dev(3))):
        b_out.append(send(w.at[second], piece(y, z, second), us.at[way], ur.at[way], to))
    w_own = pltpu.make_async_copy(w, w_all.at[yh, yl, z, core], lsem.at[0])
    w_own.start()


    def res_far():
        for way in (0, 1):
            for block in (0, 1):
                at = way * 2 + block
                r_out.append(
                    send(
                        res.at[pl.ds(way * HALF, HALF), columns(block, opposite)], transit.at[way, block],
                        rs.at[at], rr.at[at], x_dev(1 if way == 0 else 3),
                    )
                )

    def res_near(half):
        rows = pl.ds(half * HALF, HALF)
        for way in (0, 1):
            for block in (0, 1):
                at = 4 + 4 * half + 2 * way + block
                r_out.append(
                    send(
                        res.at[rows, columns(block, right if way == 0 else left)], res_in.at[x, block, rows],
                        rs.at[at], rr.at[at], x_dev(1 if way == 0 else 3),
                    )
                )

    def res_relay():
        for way in (0, 1):
            for block in (0, 1):
                at = way * 2 + block
                arrived(transit.at[way, block], rr.at[at])
                spot = res_in.at[left if way == 0 else right, block, pl.ds(way * HALF, HALF)]
                r_out.append(
                    send(transit.at[way, block], spot, rs.at[12 + at], rr.at[12 + at], x_dev(1 if way == 0 else 3))
                )

    partner = y_dev(2)
    n_out = [
        send(head, head_all.at[yh], ns.at[0], nr.at[0], partner),
        send(gain, gain_all.at[yh, 0], ns.at[1], nr.at[1], partner),
        send(bias, bias_all.at[yh, 0], ns.at[2], nr.at[2], partner),
    ]
    own = [
        pltpu.make_async_copy(ctx, ctx_all.at[x], lsem.at[1]),
        pltpu.make_async_copy(res.at[:, columns(0, x)], res_in.at[x, 0], lsem.at[2]),
        pltpu.make_async_copy(res.at[:, columns(1, x)], res_in.at[x, 1], lsem.at[3]),
        pltpu.make_async_copy(head, head_all.at[yh], lsem.at[4]),
        pltpu.make_async_copy(gain, gain_all.at[yh, 0], lsem.at[5]),
        pltpu.make_async_copy(bias, bias_all.at[yh, 0], lsem.at[6]),
        pltpu.make_async_copy(targets_in, targets, lsem.at[7]),
        pltpu.make_async_copy(packing_in, packing, lsem.at[8]),
        pltpu.make_async_copy(lens_in, lens, lsem.at[9]),
    ]
    for copy in own:
        copy.start()

    h_out, z_out = [], []

    def below(step):
        return lax.rem(z + NZ - step, NZ)

    def above(step):
        return lax.rem(z + step, NZ)

    def spots(step):
        if step == 0:
            return [(z, 0)]
        if step == 4:
            return [(below(4), 7)]
        return [(below(step), 2 * step - 1), (above(step), 2 * step)]

    def bundle(at):
        return w_all.at[:, :, at, core, first]

    def a_in(step):
        if step == 0:
            w_own.wait()
            for k in (1, 2, 3):
                arrived(piece(lax.rem(y + 4 - k, 4), z, first), wr.at[k - 1])
        elif step < 4:
            arrived(bundle(below(step)), zr.at[step - 1])
            arrived(bundle(above(step)), zr.at[4 + step - 1])
        else:
            arrived(w_all.at[0, :, below(4), core, first], zr.at[3])
            arrived(w_all.at[1, :, below(4), core, first], zr.at[7])
        if step < 3:
            up, down = bundle(below(step)), bundle(above(step))
        elif step == 3:
            up, down = w_all.at[0, :, below(3), core, first], w_all.at[1, :, above(3), core, first]
        else:
            return
        z_out.append(send(up, up, zs.at[step], zr.at[step], z_dev(1)))
        z_out.append(send(down, down, zs.at[4 + step], zr.at[4 + step], z_dev(NZ - 1)))

    def b_in(step):
        if step < 4:
            arrived(piece(y, below(step), second), br.at[step - 1])
            arrived(piece(y, above(step), second), br.at[4 + step - 1])
            up_rows, down_rows = (second, second) if step < 3 else (upper, lower)
            up, down = piece(y, below(step), up_rows), piece(y, above(step), down_rows)
            b_out.append(send(up, up, bs.at[step], br.at[step], z_dev(1)))
            b_out.append(send(down, down, bs.at[4 + step], br.at[4 + step], z_dev(NZ - 1)))
        else:
            arrived(piece(y, below(4), upper), br.at[3])
            arrived(piece(y, below(4), lower), br.at[7])
        for at, number in spots(step):
            spot = piece(y, at, second)
            b_out.append(send(spot, spot, us.at[2 * number], ur.at[2 * number], y_dev(1)))
            b_out.append(send(spot, spot, us.at[2 * number + 1], ur.at[2 * number + 1], y_dev(3)))

    def relay(step):
        for at, number in spots(step):
            for way, frm, rows in ((0, lax.rem(y + 3, 4), upper), (1, lax.rem(y + 1, 4), lower)):
                arrived(piece(frm, at, second), ur.at[2 * number + way])
                spot = piece(frm, at, rows)
                b_out.append(
                    send(spot, spot, os.at[2 * number + way], or_.at[2 * number + way], y_dev(1 if way == 0 else 3))
                )

    def hand(step):
        for at, number in spots(step):
            for way, rows in ((0, upper), (1, lower)):
                arrived(piece(lax.rem(y + 2, 4), at, rows), or_.at[2 * number + way])
            whole = w_all.at[:, :, at, core]
            h_out.append(send(whole, whole, hs.at[number], hr.at[number], sibling))

    def handed(step):
        for at, number in spots(step):
            arrived(w_all.at[:, :, at, 1 - core], hr.at[number])

    def multiply(pair, start):
        @pl.loop(0, LOCAL_WIDTH // 256)
        def _(n):
            block, at = n // 5, lax.rem(n, 5)
            cols = pl.ds(pl.multiple_of(at * 256, 256), 256)
            a = jnp.concatenate(
                [
                    ctx_all[:, :, pl.ds(pl.multiple_of((low * 4 + pair) * PAIR, PAIR), PAIR)].reshape(NX * ROWS, PAIR)
                    for low in (0, 1)
                ],
                axis=1,
            )
            b = jnp.concatenate(
                [w_all[block, low, pl.ds(pair * 2, 2), :, :, cols].reshape(PAIR, 256) for low in (0, 1)], axis=0
            )
            total = jnp.dot(a, b, preferred_element_type=F32)
            if start:
                hid[block, :, cols] = total
            else:
                hid[block, :, cols] += total

    a_in(0)
    b_in(1)
    relay(0)

    a_in(1)
    b_in(2)

    arrived(ctx_part(ctx_all.at[left], 0), cr.at[0])
    c_out.append(
        send(ctx_part(ctx_all.at[left], 0), ctx_part(ctx_all.at[left], 0), cs.at[4], cr.at[4], x_dev(1))
    )
    arrived(ctx_part(ctx_all.at[right], 1), cr.at[3])
    c_out.append(
        send(ctx_part(ctx_all.at[right], 1), ctx_part(ctx_all.at[right], 1), cs.at[5], cr.at[5], x_dev(3))
    )
    relay(1)
    hand(0)

    own[3].wait()
    own[4].wait()
    own[5].wait()
    arrived(head_all.at[1 - yh], nr.at[0])
    arrived(gain_all.at[1 - yh, 0], nr.at[1])
    arrived(bias_all.at[1 - yh, 0], nr.at[2])
    g_row = jnp.zeros((8, VOCAB), F32)
    for block in (0, 1):
        lhs = jnp.concatenate(
            [
                jnp.broadcast_to(gain_all[block], (4, NB)),
                jnp.broadcast_to(bias_all[block], (4, NB)),
            ],
            axis=0,
        )
        for _ in range(3):
            top = lhs.astype(BF16)
            g_row += jnp.dot(top, head_all[block], preferred_element_type=F32)
            lhs = lhs - top.astype(F32)
    g_own[...] = g_row
    g_out = [send(g_own, g_in.at[k], gs.at[k], gr.at[k], x_dev(k + 1)) for k in range(3)]

    a_in(2)
    b_in(3)
    for copy in c_out[:4]:
        copy.wait_send()
    res_far()
    relay(2)
    hand(1)
    for copy in c_out[4:]:
        copy.wait_send()
    res_near(0)
    a_in(3)
    b_in(4)
    own[0].wait()
    arrived(ctx_part(ctx_all.at[left], 1), cr.at[1])
    arrived(ctx_part(ctx_all.at[right], 0), cr.at[2])
    arrived(ctx_part(ctx_all.at[opposite], 0), cr.at[4])
    arrived(ctx_part(ctx_all.at[opposite], 1), cr.at[5])
    relay(3)
    hand(2)

    base = z // 2
    odd = lax.rem(z, 2)
    handed(0)
    handed(1)
    multiply(base, True)
    res_relay()
    a_in(4)
    relay(4)
    hand(3)
    handed(2)
    multiply(lax.rem(base + 3 + 2 * odd, 4), False)
    res_near(1)
    hand(4)
    handed(3)
    multiply(lax.rem(base + 1 + 2 * odd, 4), False)
    handed(4)
    multiply(lax.rem(base + 2, 4), False)

    def half_block(k, half):
        rows_of = lax.rem(x + k + 1, NX)
        at = pl.ds(pl.multiple_of(rows_of * ROWS + half * HALF, HALF), HALF)
        within = pl.ds(half * HALF, HALF)
        row_sum = jnp.zeros((HALF, 1), F32)
        for block in (0, 1):
            full = hid[block, at] + res_in[rows_of, block, within].astype(F32)
            hid[block, at] = full
            row_sum += jnp.sum(full, axis=1, keepdims=True)
        mean = row_sum * (1.0 / LOCAL_WIDTH)
        square = jnp.zeros((HALF, 1), F32)
        product = jnp.zeros((2 * HALF, VOCAB), F32)
        for block in (0, 1):
            off = hid[block, at] - mean
            square += jnp.sum(off * off, axis=1, keepdims=True)
            scaled = off * gain_all[block]
            top = scaled.astype(BF16)
            rest = (scaled - top.astype(F32)).astype(BF16)
            product += jnp.dot(
                jnp.concatenate([top, rest], axis=0), head_all[block], preferred_element_type=F32
            )
        lane = lax.broadcasted_iota(jnp.int32, (HALF, VOCAB), 1)
        both = jnp.concatenate(
            [jnp.where(lane == 0, mean, square), jnp.zeros((VOCAB - HALF, VOCAB), F32)], axis=0
        )
        part[k, half, :HALF] = product[:HALF] + product[HALF:]
        part[k, half, HALF:] = jnp.transpose(both)[:8]
        if k < 3:
            p_out.append(
                send(part.at[k, half], part_in.at[k, half], ps.at[2 * k + half], pr.at[2 * k + half], x_dev(k + 1))
            )

    p_out = []
    for copy in own[1:3] + own[6:]:
        copy.wait()
    for half in (0, 1):
        half_block(3, half)
    for copy in w_out + n_out + z_out + b_out + h_out + g_out:
        copy.wait_send()
    for half in (0, 1):
        for block in (0, 1):
            arrived(res_in.at[opposite, block, pl.ds(half * HALF, HALF)], rr.at[12 + 2 * half + block])
        half_block(1, half)
    for half in (0, 1):
        for way in (0, 1):
            for block in (0, 1):
                arrived(
                    res_in.at[left if way == 0 else right, block, pl.ds(half * HALF, HALF)],
                    rr.at[4 + 4 * half + 2 * way + block],
                )
            half_block(2 if way == 0 else 0, half)

    info[...] = jnp.full((8, 256), -1, jnp.int32)
    info[0:1, :ROWS] = targets[...].reshape(1, ROWS)
    info[1:3, :ROWS] = packing[...]
    label = jnp.transpose(jnp.broadcast_to(info[0:1, :].astype(F32), (VOCAB, 256)))[:ROWS]
    group = info[1:2, :]
    place = info[2:3, :]
    chosen = jnp.where(lax.broadcasted_iota(jnp.int32, (VOCAB, 256), 0) == place, 1.0, 0.0).astype(BF16)
    to_group = lax.broadcasted_iota(jnp.int32, (NDP, 256), 0) == group
    for k in range(3):
        arrived(g_in.at[k], gr.at[k])
    sums = [g_own[...]] + [g_in[k] for k in range(3)]
    shift = sums[0][4:5] + sums[1][4:5] + sums[2][4:5] + sums[3][4:5]
    token = lax.broadcasted_iota(jnp.int32, (HALF, VOCAB), 1).astype(F32)

    def score_of(half):
        for k in range(3):
            arrived(part_in.at[k, half], pr.at[2 * k + half])
        parts = [part[3, half]] + [part_in[k, half] for k in range(3)]
        stats = [p[HALF:] for p in parts]
        center = (stats[0][0:1] + stats[1][0:1] + stats[2][0:1] + stats[3][0:1]) * 0.25
        total_square = stats[0][1:2] + stats[1][1:2] + stats[2][1:2] + stats[3][1:2]
        away = [st[0:1] - center for st in stats]
        for a in away:
            total_square += LOCAL_WIDTH * (a * a)
        inverse = lax.rsqrt(total_square * (1.0 / WIDTH) + EPS)
        by_row = jnp.transpose(jnp.concatenate([inverse, *away, jnp.zeros((VOCAB - 5, VOCAB), F32)], axis=0))[:HALF]
        logits = jnp.zeros((HALF, VOCAB), F32)
        for i in range(4):
            logits += parts[i][:HALF] + by_row[:, i + 1 : i + 2] * sums[i][0:1]
        logits = logits * by_row[:, 0:1] + shift
        largest = jnp.max(logits, axis=1, keepdims=True)
        log_total = largest + jnp.log(jnp.sum(jnp.exp(logits - largest), axis=1, keepdims=True))
        wanted = label[half * HALF : (half + 1) * HALF]
        picked = jnp.sum(jnp.where(token == wanted, logits, 0.0), axis=1, keepdims=True)
        return jnp.broadcast_to(picked - log_total, (HALF, VOCAB))

    score = [score_of(0), score_of(1)]
    score_rows = jnp.transpose(jnp.concatenate(score + [jnp.zeros((256 - ROWS, VOCAB), F32)], axis=0))

    lhs = jnp.where(to_group, score_rows[:NDP], 0.0)
    packed = jnp.zeros((NDP, VOCAB), F32)
    for _ in range(3):
        top = lhs.astype(BF16)
        packed += lax.dot_general(top, chosen, (((1,), (1,)), ((), ())), preferred_element_type=F32)
        lhs = lhs - top.astype(F32)
    dp_send[...] = packed.reshape(NDP, 1, VOCAB)

    def deliver(k):
        to = lax.rem(dp + k, NDP)
        send(dp_send.at[to], dp_in.at[k - 1], ds_.at[0], dr.at[0], (to, tensor))

    pl.loop(8, NDP)(deliver)
    pl.loop(1, 8)(deliver)

    live_score = jnp.where(group >= 0, score_rows[0:1], 0.0)
    out[0:1] = live_score
    at_row = lax.broadcasted_iota(jnp.int32, (1, 256), 1)
    lane = lax.broadcasted_iota(jnp.int32, (1, VOCAB), 1)
    begin = jnp.int32(0)
    proteins = jnp.zeros((1, VOCAB), F32)
    for i in range(4):
        length = lens[i]
        end = begin + length
        inside = jnp.where((at_row >= begin) & (at_row < end), live_score, 0.0)
        one = jnp.sum(inside, axis=1, keepdims=True) / jnp.broadcast_to(
            jnp.maximum(length, 1).astype(F32), (1, 1)
        )
        proteins = jnp.where(lane == i, one, proteins)
        begin = end
    out[2:3, :VOCAB] = proteins

    for copy in r_out + p_out:
        copy.wait_send()
    arrived(dp_in, dr.at[0])
    arrived(dp_in, ds_.at[0])
    packed_row = dp_send[dp] + jnp.sum(dp_in[...], axis=0)
    out[1:2, :VOCAB] = packed_row


def deal(rows, scores, packed, proteins):
    scores[...] = rows[0:1, :ROWS].reshape(ROWS)
    packed[...] = rows[1:2, :HALF].reshape(HALF)
    proteins[...] = rows[2:3, :4].reshape(4)


def shards(context, residual, out_weight, norm_gain, norm_bias, head_weight, targets, packing, lengths):
    any_ = pl.BlockSpec(memory_space=pl.ANY)
    vmem = pl.BlockSpec(memory_space=pltpu.VMEM)
    dma = pltpu.SemaphoreType.DMA
    rows = pl.pallas_call(
        kernel,
        out_shape=jax.ShapeDtypeStruct((8, 256), F32),
        in_specs=[any_] * 9,
        out_specs=vmem,
        scratch_shapes=[
            pltpu.VMEM((NX, ROWS, CTX), BF16),
            pltpu.VMEM((NX, 2, ROWS, NB), BF16),
            pltpu.VMEM((2, 2, HALF, NB), BF16),
            pltpu.VMEM((2, 2, NZ, 2, KB, NB), BF16),
            pltpu.VMEM((2, NX * ROWS, NB), F32),
            pltpu.VMEM((2, NB, VOCAB), BF16),
            pltpu.VMEM((2, 1, NB), F32),
            pltpu.VMEM((2, 1, NB), F32),
            pltpu.VMEM((8, VOCAB), F32),
            pltpu.VMEM((3, 8, VOCAB), F32),
            pltpu.VMEM((4, 2, HALF + 8, VOCAB), F32),
            pltpu.VMEM((3, 2, HALF + 8, VOCAB), F32),
            pltpu.VMEM((8, 256), jnp.int32),
            pltpu.VMEM((ROWS,), jnp.int32),
            pltpu.VMEM((2, ROWS), jnp.int32),
            pltpu.SMEM((4,), jnp.int32),
            pltpu.VMEM((NDP, 1, VOCAB), F32),
            pltpu.VMEM((NDP - 1, 1, VOCAB), F32),
            dma((10,)),
            dma((6,)), dma((6,)),
            dma((16,)), dma((16,)),
            dma((3,)), dma((3,)),
            dma((8,)), dma((8,)),
            dma((8,)), dma((8,)),
            dma((16,)), dma((16,)),
            dma((16,)), dma((16,)),
            dma((8,)), dma((8,)),
            dma((3,)), dma((3,)),
            dma((3,)), dma((3,)),
            dma((6,)), dma((6,)),
            dma((1,)), dma((1,)),
        ],
        compiler_params=pltpu.CompilerParams(
            collective_id=0, has_side_effects=True, vmem_limit_bytes=60 * 2**20
        ),
    )(
        context, residual, out_weight, head_weight,
        norm_gain, norm_bias, targets, packing, lengths,
    )
    return pl.pallas_call(
        deal,
        out_shape=tuple(jax.ShapeDtypeStruct((n,), F32) for n in (ROWS, HALF, 4)),
        in_specs=[vmem],
        out_specs=(vmem, vmem, vmem),
    )(rows)


def solution(mesh):
    placed = (
        P(("dp", "tensor"), None),
        P(("dp", "tensor"), None),
        P("dp", "tensor"),
        P("tensor"),
        P("tensor"),
        P("tensor", None),
        P(("dp", "tensor")),
        P(None, ("dp", "tensor")),
        P(("dp", "tensor")),
    )
    rows = P(("dp", "tensor"))
    return jax.shard_map(shards, mesh=mesh, in_specs=placed, out_specs=(rows, rows, rows), check_vma=False)
```
